32 devices in a mesh: view: 8 (over z, y), row: 4 (over x, core).
Axes of the slice: x: 2, y: 2, z: 4, core: 2. Of those that a mesh axis runs over, the one named last changes fastest.
Arguments:
- latent: bfloat16 [1, 8, 8, 72, 1280], P(None, 'view', 'row'), may hold values from -30 to 30
- gn_gain: float32 [1280], replicated, may hold values from 0.25 to 1.75
- gn_bias: float32 [1280], replicated, may hold values from -3 to 3
- cam_idx: int32 [1, 8], P(None, 'view'), may hold values from 0 to 63
- noise_idx: int32 [1], replicated, may hold values from 0 to 999
- cam_table: bfloat16 [64, 2560], replicated, may hold values from -2 to 2
- noise_table: bfloat16 [1000, 2560], replicated, may hold values from -2 to 2
- conv_w: bfloat16 [3, 3, 1280, 1280], P(None, None, None, 'row'), may hold values from -0.0546875 to 0.0546875
- conv_bias: float32 [1280], replicated, may hold values from -3 to 3
- ln_gain: float32 [1280], replicated, may hold values from 0.25 to 1.75
- attn_in: bfloat16 [3, 1280, 1280], P(None, None, 'view'), may hold values from -0.15625 to 0.15625
- attn_out: bfloat16 [1280, 1280], P('view'), may hold values from -0.15625 to 0.15625
- head_scale: float32 [20], replicated, may hold values from 0.4 to 135
Outputs:
- block_out: bfloat16 [1, 8, 8, 72, 1280], P(None, 'view', 'row')
The draws below stay inside these ranges and needn't reach their ends.
All inputs are finite; a program needn't handle non-finite values.
Results may differ from the reference program's by a relative error of at most 0.02.
Values may be sent and summed in bfloat16 or wider, within the bound.
A program may use at most 192 MiB of HBM per device.

```python
import math
import jax
import jax.numpy as jnp
from jax import lax

C = 1280
HEADS = 20
HD = 64
GROUPS = 32
WIDTH = 72
NCAM = 64
NLEVEL = 1000
SAMPLES = 1
CO = 1280
VIEWS = 8
HEIGHT = 8


def draw_latent(key, part):
    normal_part = jnp.clip(jax.random.normal(key, (SAMPLES, VIEWS, HEIGHT, WIDTH, C), jnp.float32), -3.5, 3.5)
    row_ramp = 1.0 + 2.0 * jnp.arange(HEIGHT, dtype=jnp.float32) / max(HEIGHT - 1, 1)
    row_ramp = row_ramp[None, None, :, None, None]
    offset = jax.random.uniform(jax.random.fold_in(key, 11), (C,), jnp.float32, 0.4, 1.0)
    return (normal_part * row_ramp + offset * row_ramp).astype(jnp.bfloat16)


def draw_head_scale(key, part):
    ladder = jnp.exp(jnp.linspace(math.log(0.5), math.log(2.0), HEADS))
    order_perm = jax.random.permutation(jax.random.fold_in(key, 3), HEADS)
    jitter = jax.random.uniform(jax.random.fold_in(key, 5), (HEADS,), jnp.float32, 0.9, 1.1)
    return ladder[order_perm] * jitter


def touch_ends(array, own_key, smallest, largest):
    longest = array.shape.index(max(array.shape))
    spots = []
    for shift in (0, 1):
        where = [jax.random.randint(jax.random.fold_in(own_key, axis), (), 0, length) for axis, length in enumerate(array.shape)]
        where[longest] = (where[longest] + shift) % array.shape[longest]
        spots.append(tuple(where))
    return array.at[spots[0]].set(smallest).at[spots[1]].set(largest)


def shard_levels(rng, dims, split, low, largest):
    gain, own = 1.0, jax.random.fold_in(rng, 6)
    for dim, parts in split:
        heights = jnp.exp(jax.random.uniform(jax.random.fold_in(own, dim), (parts,), jnp.float32, low / len(split), largest / len(split)))
        gain = gain * jnp.repeat(heights, dims[dim] // parts).reshape([-1 if axis == dim else 1 for axis in range(len(dims))])
    return gain


def gaussian(key, dims, deviation, reach, split=(), kind=jnp.bfloat16):
    values = jax.random.normal(key, dims, jnp.float32) * deviation
    if len(split) > 0:
        values = shard_levels(key, dims, split, -0.22, 0.18) * values
    return jnp.clip(values, min=-reach, max=reach).astype(kind)


def setup_inputs(seed: int = 0) -> dict:
    seeds = jax.random.split(jax.random.key(seed), 14)
    return {
        "latent": draw_latent(jax.random.fold_in(seeds[13], 71), 0),
        "gn_gain": jnp.clip(1.0 + 0.15 * jax.random.normal(seeds[1], (C,), jnp.float32), 0.25, 1.75),
        "gn_bias": gaussian(seeds[2], (C,), 0.5, 3.0, (), jnp.float32),
        "cam_idx": touch_ends(jax.random.randint(seeds[3], (SAMPLES, VIEWS), 0, NCAM), jax.random.fold_in(seeds[3], 1), 0, NCAM - 1).astype(jnp.int32),
        "noise_idx": jax.random.randint(seeds[4], (SAMPLES,), 0, NLEVEL).astype(jnp.int32),
        "cam_table": gaussian(seeds[5], (NCAM, 2 * C), 0.4, 2.0),
        "noise_table": gaussian(seeds[6], (NLEVEL, 2 * C), 0.4, 2.0),
        "conv_w": gaussian(seeds[7], (3, 3, C, CO), (9 * C) ** -0.5, 0.0546875, ((3, 4),)),
        "conv_bias": gaussian(seeds[8], (CO,), 0.5, 3.0, (), jnp.float32),
        "ln_gain": jnp.clip(1.0 + 0.15 * jax.random.normal(seeds[9], (CO,), jnp.float32), 0.25, 1.75),
        "attn_in": gaussian(seeds[10], (3, CO, CO), CO ** -0.5, 0.15625, ((2, 8),)),
        "attn_out": gaussian(seeds[11], (CO, CO), CO ** -0.5, 0.15625, ((0, 8),)),
        "head_scale": draw_head_scale(jax.random.fold_in(seeds[13], 71), 0),
    }


epsilon = 1e-05

def reference(latent, gn_gain, gn_bias, cam_idx, noise_idx, cam_table, noise_table, conv_w, conv_bias, ln_gain, attn_in, attn_out, head_scale):
    x_float = latent.astype(jnp.float32)
    grouped = x_float.reshape(SAMPLES, VIEWS, HEIGHT, WIDTH, GROUPS, C // GROUPS)
    average = lax.optimization_barrier(jnp.mean(grouped, axis=(2, 3, 5), keepdims=True))
    centred = grouped - average
    variance = lax.optimization_barrier(jnp.mean(centred * centred, axis=(2, 3, 5), keepdims=True))
    normed = (centred * lax.rsqrt(variance + epsilon)).reshape(x_float.shape)
    film_rows = cam_table[cam_idx].astype(jnp.float32) + noise_table[noise_idx].astype(jnp.float32)[:, None, :]
    film_scale = film_rows[:, :, None, None, :C]
    film_shift = film_rows[:, :, None, None, C:]
    hidden = (normed * gn_gain + gn_bias) * (1.0 + film_scale) + film_shift
    activated = jax.nn.silu(hidden).astype(jnp.bfloat16)
    padded = jnp.pad(activated, ((0, 0), (0, 0), (1, 1), (1, 1), (0, 0)))
    conv_out = jnp.zeros((SAMPLES * VIEWS * HEIGHT * WIDTH, CO), jnp.float32)
    for tap_row in range(3):
        for tap_col in range(3):
            tap_rows = padded[:, :, tap_row:tap_row + HEIGHT, tap_col:tap_col + WIDTH, :].reshape(-1, C)
            conv_out = conv_out + jnp.dot(tap_rows, conv_w[tap_row, tap_col], preferred_element_type=jnp.float32)
    conv_out = conv_out.reshape(SAMPLES, VIEWS, HEIGHT, WIDTH, CO)
    resid_out = (x_float + conv_out + conv_bias).astype(jnp.bfloat16)
    resid_float = resid_out.astype(jnp.float32)
    middle = lax.optimization_barrier(jnp.mean(resid_float, axis=-1, keepdims=True))
    spread = lax.optimization_barrier(jnp.mean((resid_float - middle) ** 2, axis=-1, keepdims=True))
    normed_y = ((resid_float - middle) * lax.rsqrt(spread + epsilon) * ln_gain).astype(jnp.bfloat16)
    flat_y = normed_y.reshape(-1, CO)
    head_shape = (SAMPLES, VIEWS, HEIGHT * WIDTH, HEADS, HD)
    query = jnp.dot(flat_y, attn_in[0], preferred_element_type=jnp.float32).astype(jnp.bfloat16).reshape(head_shape)
    key_heads = jnp.dot(flat_y, attn_in[1], preferred_element_type=jnp.float32).astype(jnp.bfloat16).reshape(head_shape)
    value = jnp.dot(flat_y, attn_in[2], preferred_element_type=jnp.float32).astype(jnp.bfloat16).reshape(head_shape)
    scores = jnp.einsum('svphd,suphd->sphvu', query.astype(jnp.float32), key_heads.astype(jnp.float32))
    scores = scores * (head_scale / math.sqrt(HD))[None, None, :, None, None]
    peak_score = lax.optimization_barrier(jnp.max(scores, axis=-1, keepdims=True))
    exp_scores = jnp.exp(scores - peak_score)
    soft_weights = (exp_scores / lax.optimization_barrier(jnp.sum(exp_scores, axis=-1, keepdims=True))).astype(jnp.bfloat16)
    mixed = jnp.einsum('sphvu,suphd->svphd', soft_weights.astype(jnp.float32), value.astype(jnp.float32)).astype(jnp.bfloat16)
    projected = jnp.dot(mixed.reshape(-1, CO), attn_out, preferred_element_type=jnp.float32)
    return (resid_float + projected.reshape(resid_float.shape)).astype(jnp.bfloat16)
```

```python
import functools
import math

import jax
import jax.numpy as jnp
from jax import lax
from jax.experimental import pallas as pl
from jax.experimental.pallas import tpu as pltpu
from jax.sharding import PartitionSpec as P

GROUPS = 32
EPS = 1e-05
F32 = jnp.float32
BF16 = jnp.bfloat16
HIGHEST = lax.Precision.HIGHEST


def up(n, m):
    return (n + m - 1) // m * m


def one_hot(shape, long_axis, size):
    long = lax.broadcasted_iota(jnp.int32, shape, long_axis)
    short = lax.broadcasted_iota(jnp.int32, shape, 1 - long_axis) * size
    return (long >= short) & (long < short + size)


def kernel(
    dims,
    x_ref,
    film_ref,
    affine_ref,
    scale_ref,
    conv_hbm,
    attn_hbm,
    resid_ref,
    mixed_ref,
    stat,
    act,
    conv_w,
    acc,
    conv_s,
    conv_r,
    attn_w,
    ny,
    ally,
    qkv,
    mix_s,
    mix_r,
    load_sem,
    stat_ss,
    stat_rs,
    act_ss,
    act_rs,
    fwd_ss,
    fwd_rs,
    conv_ss,
    conv_rs,
    attn_ss,
    attn_rs,
    attn_fs,
    attn_fr,
    pair_ss,
    pair_rs,
    line_ss,
    line_rs,
    mix_ss,
    mix_rs,
):
    V, R, H, g, T, rows, W, Wp, C, head = dims
    B = rows * Wp
    Cr = conv_w.shape[-1]
    v = lax.axis_index("view")
    r = lax.axis_index("row")
    h = v // g
    q = v % g
    core = r % 2
    sib = r + 1 - 2 * core

    def at(view=None, row=None):
        return (v if view is None else view, r if row is None else row)

    def remote(src, dst, ss, rs, device):
        return pltpu.make_async_remote_copy(
            src_ref=src,
            dst_ref=dst,
            send_sem=ss,
            recv_sem=rs,
            device_id=device,
            device_id_type=pl.DeviceIdType.MESH,
        )

    load_conv = pltpu.make_async_copy(conv_hbm, conv_w, load_sem.at[0])
    load_conv.start()
    load_attn = pltpu.make_async_copy(attn_hbm, attn_w.at[q], load_sem.at[1])
    load_attn.start()

    barrier = pltpu.get_barrier_semaphore()
    for o in range(1, R):
        pl.semaphore_signal(
            barrier, inc=1, device_id=at(row=(r + o) % R), device_id_type=pl.DeviceIdType.MESH
        )
    for o in range(1, V):
        pl.semaphore_signal(
            barrier, inc=1, device_id=at(view=(v + o) % V), device_id_type=pl.DeviceIdType.MESH
        )

    x = x_ref[...].astype(F32).reshape(rows * W, C)
    size = C // GROUPS
    into = one_hot((C, 128), 0, size).astype(F32)
    back = one_hot((128, C), 1, size).astype(F32)
    count = rows * W * size

    def spread(total):
        total = jnp.broadcast_to(total, (8, C))
        grouped = jnp.dot(total, into, precision=HIGHEST, preferred_element_type=F32)
        return jnp.dot(grouped, back, precision=HIGHEST, preferred_element_type=F32)[0:1]

    mean_here = spread(jnp.sum(x, axis=0, keepdims=True)) * (1.0 / count)
    off = x - mean_here
    square_here = spread(jnp.sum(off * off, axis=0, keepdims=True))
    stat[r, 0:1, :] = mean_here
    stat[r, 1:2, :] = square_here

    pl.semaphore_wait(barrier, R - 1 + V - 1)

    stat_copies = []
    for o in range(1, R):
        copy = remote(
            stat.at[r], stat.at[r], stat_ss.at[o], stat_rs.at[o], at(row=(r + o) % R)
        )
        copy.start()
        stat_copies.append(copy)

    half = C // 2
    mine = pl.ds(pl.multiple_of(core * half, half), half)
    attn_copies = []
    for o in range(1, g):
        copy = remote(
            attn_hbm.at[:, mine, :],
            attn_w.at[q, :, mine, :],
            attn_ss.at[o],
            attn_rs.at[o],
            at(view=h * g + (q + o) % g),
        )
        copy.start()
        attn_copies.append(copy)

    act[0:Wp, :] = jnp.zeros((Wp, C), BF16)
    act[Wp + R * B : 2 * Wp + R * B, :] = jnp.zeros((Wp, C), BF16)

    for copy in stat_copies:
        copy.wait()
    means = [stat[d, 0:1, :] for d in range(R)]
    mean = sum(means[1:], means[0]) * (1.0 / R)
    total = jnp.zeros((1, C), F32)
    for d in range(R):
        gap = means[d] - mean
        total = total + stat[d, 1:2, :] + count * (gap * gap)
    rstd = lax.rsqrt(total * (1.0 / (count * R)) + EPS)
    gain = rstd * film_ref[0:1, :]
    hidden = (x - mean) * gain + film_ref[1:2, :]
    hidden = hidden / (1.0 + jnp.exp(-hidden))

    def pad(values):
        parts = []
        for i in range(rows):
            parts.append(values[i * W : (i + 1) * W])
            parts.append(jnp.zeros((Wp - W, C), F32))
        return jnp.concatenate(parts, axis=0)

    def block(d):
        return act.at[pl.ds(pl.multiple_of(Wp + B * d, 16), B), :]

    act[pl.ds(pl.multiple_of(Wp + B * r, 16), B), :] = pad(hidden).astype(BF16)

    act_copies = []
    for o in range(1, R // 2):
        copy = remote(
            block(r), block(r), act_ss.at[o], act_rs.at[o], at(row=(r + 2 * o) % R)
        )
        copy.start()
        act_copies.append(copy)
    forwards = [remote(block(r), block(r), fwd_ss.at[0], fwd_rs.at[0], at(row=sib))]
    forwards[0].start()
    for o in range(1, R // 2):
        act_copies[o - 1].wait_recv()
        source = (r + R - 2 * o) % R
        copy = remote(
            block(source), block(source), fwd_ss.at[o], fwd_rs.at[o], at(row=sib)
        )
        copy.start()
        forwards.append(copy)
    for copy in act_copies:
        copy.wait_send()
    load_conv.wait()
    for copy in forwards:
        copy.wait()

    M = acc.shape[1]

    def chunk(m, carry):
        start = pl.multiple_of(m * M, 16)
        for tap in range(3):
            acc[tap] = jnp.zeros((M, Cr), F32)

        def taps(t, carry):
            i = t // 3
            j = t % 3
            lines = act[pl.ds(pl.multiple_of(start + i * Wp, 16), M), :]
            acc[j] += jnp.dot(lines, conv_w[t], preferred_element_type=F32)
            return carry

        lax.fori_loop(0, 9, taps, 0)
        left = acc[0]
        left = jnp.concatenate([left[M - 1 :], left[: M - 1]], axis=0)
        right = acc[2]
        right = jnp.concatenate([right[1:], right[:1]], axis=0)
        conv_s[pl.ds(start, M), :] = (left + acc[1] + right).astype(BF16)
        return carry

    lax.fori_loop(0, R * B // M, chunk, 0)

    conv_copies = []
    for o in range(1, R):
        to = (r + o) % R
        copy = remote(
            conv_s.at[pl.ds(pl.multiple_of(B * to, 16), B), :],
            conv_r.at[r],
            conv_ss.at[o],
            conv_rs.at[o],
            at(row=to),
        )
        copy.start()
        conv_copies.append(copy)
    conv_r[r] = conv_s[pl.ds(pl.multiple_of(B * r, 16), B), :]

    attn_forwards = []
    for o in range(1, g):
        attn_copies[o - 1].wait()
        source = (q + g - o) % g
        copy = remote(
            attn_w.at[source, :, mine, :],
            attn_w.at[source, :, mine, :],
            attn_fs.at[o],
            attn_fr.at[o],
            at(row=sib),
        )
        copy.start()
        attn_forwards.append(copy)

    for copy in conv_copies:
        copy.wait()
    conv = jnp.concatenate([conv_r[d].astype(F32) for d in range(R)], axis=1)
    resid = (pad(x_ref[...].astype(F32).reshape(rows * W, C)) + conv + affine_ref[0:1, :]).astype(
        BF16
    )
    for i in range(rows):
        resid_ref[i] = resid[i * Wp : i * Wp + W]
    resid = resid.astype(F32)
    middle = jnp.mean(resid, axis=1, keepdims=True)
    gap = resid - middle
    var = jnp.mean(gap * gap, axis=1, keepdims=True)
    ny[0:B, :] = (gap * lax.rsqrt(var + EPS) * affine_ref[1:2, :]).astype(BF16)
    if g * T > B:
        ny[B : g * T, :] = jnp.zeros((g * T - B, C), BF16)

    def share(k):
        return pl.ds(pl.multiple_of(k * T, 16), T)

    ally[h, q] = ny[share(q), :]
    pair_copies = []
    for o in range(1, g):
        to = (q + o) % g
        copy = remote(
            ny.at[share(to), :], ally.at[h, q], pair_ss.at[o], pair_rs.at[o], at(view=h * g + to)
        )
        copy.start()
        pair_copies.append(copy)

    def hop(way, s, o):
        step = 1 - 2 * way
        origin = h - s if way == 0 else h + s
        target = h + step
        valid = (origin >= 0) & (target < H) if way == 0 else (origin < H) & (target >= 0)
        origin = jnp.clip(origin, 0, H - 1)
        target = jnp.clip(target, 0, H - 1)
        part = ally.at[origin, (q + g - o) % g]
        copy = remote(
            part, part, line_ss.at[way, s, o], line_rs.at[way, s, o], at(view=target * g + q)
        )
        return valid, copy

    def arrives(way, s):
        return h - 1 - s >= 0 if way == 0 else h + 1 + s < H

    def await_hop(way, s, o):
        @pl.when(arrives(way, s))
        def _():
            origin = h - 1 - s if way == 0 else h + 1 + s
            part = ally.at[jnp.clip(origin, 0, H - 1), (q + g - o) % g]
            remote(
                part, part, line_ss.at[way, s, o], line_rs.at[way, s, o], at(view=(v + 1) % V)
            ).wait_recv()

    for s in range(H - 1):
        for o in range(g):
            if s == 0 and o > 0:
                pair_copies[o - 1].wait_recv()
            for way in range(2):
                if s > 0:
                    await_hop(way, s - 1, o)
                valid, copy = hop(way, s, o)

                @pl.when(valid)
                def _():
                    copy.start()

    for copy in pair_copies:
        copy.wait_send()
    load_attn.wait()
    for copy in attn_forwards:
        copy.wait()
    for o in range(g):
        for way in range(2):
            await_hop(way, H - 2, o)
            for s in range(H - 1):
                valid, copy = hop(way, s, o)

                @pl.when(valid)
                def _():
                    copy.wait_send()

    width = qkv.shape[-1]
    everything = ally[...].reshape(V * T, C)
    for kind in range(3):
        parts = [
            jnp.dot(everything, attn_w[k, kind], preferred_element_type=F32) for k in range(g)
        ]
        qkv[kind] = jnp.concatenate(parts, axis=1).astype(BF16).astype(F32)

    into_heads = one_hot((width, 128), 0, head).astype(BF16)
    from_heads = one_hot((128, width), 1, head).astype(BF16)
    scale = scale_ref[pl.ds(h, 1), :]

    def attend(k, carry):
        u = (v + 1 + k) % V
        query = qkv[0, pl.ds(pl.multiple_of(u * T, 16), T), :]
        product = (query[None] * qkv[1].reshape(V, T, width)).reshape(V * T, width)
        top = product.astype(BF16)
        low = (product - top.astype(F32)).astype(BF16)
        scores = jnp.dot(top, into_heads, preferred_element_type=F32) + jnp.dot(
            low, into_heads, preferred_element_type=F32
        )
        scores = (scores * scale).reshape(V, T, 128)
        weights = jnp.exp(scores - jnp.max(scores, axis=0, keepdims=True))
        weights = weights / jnp.sum(weights, axis=0, keepdims=True)
        weights = jnp.dot(
            weights.reshape(V * T, 128).astype(BF16), from_heads, preferred_element_type=F32
        )
        mixed = jnp.sum((weights * qkv[2]).reshape(V, T, width), axis=0).astype(BF16)

        @pl.when(u == v)
        def _():
            mix_r[h, share(q), :] = mixed

        @pl.when(u != v)
        def _():
            mix_s[u] = mixed
            remote(
                mix_s.at[u],
                mix_r.at[h, share(q), :],
                mix_ss.at[u],
                mix_rs.at[v],
                at(view=u),
            ).start()

        return carry

    lax.fori_loop(0, V, attend, 0)

    def finish(k, carry):
        u = (v + 1 + k) % V
        remote(
            mix_s.at[u],
            mix_r.at[u // g, share(u % g), :],
            mix_ss.at[u],
            mix_rs.at[u],
            at(view=u),
        ).wait()
        return carry

    lax.fori_loop(0, V - 1, finish, 0)
    mixed = jnp.concatenate([mix_r[k].astype(F32) for k in range(H)], axis=1).astype(BF16)
    for i in range(rows):
        mixed_ref[i] = mixed[i * Wp : i * Wp + W]


def local(
    latent,
    gn_gain,
    gn_bias,
    cam_idx,
    noise_idx,
    cam_table,
    noise_table,
    conv_w,
    conv_bias,
    ln_gain,
    attn_in,
    attn_out,
    head_scale,
):
    _, _, rows, W, C = latent.shape
    V = lax.axis_size("view")
    R = lax.axis_size("row")
    heads = head_scale.shape[0]
    head = C // heads
    H = math.gcd(V, heads)
    g = V // H
    Wp = up(W + 1, 16)
    B = rows * Wp
    T = up(-(-B // g), 16)
    Cr = conv_w.shape[-1]
    width = C // H
    M = math.gcd(R, 4) * B

    film = lax.dynamic_slice_in_dim(cam_table, cam_idx[0, 0], 1, 0).astype(
        F32
    ) + lax.dynamic_slice_in_dim(noise_table, noise_idx[0], 1, 0).astype(F32)
    film = film.reshape(2, C)
    gain = 1.0 + film[0]
    film = jnp.stack([gn_gain * gain, gn_bias * gain + film[1]])
    affine = jnp.stack([conv_bias, ln_gain])
    scale = jnp.pad(
        (head_scale * (1.0 / math.sqrt(head))).reshape(H, heads // H),
        ((0, 0), (0, 128 - heads // H)),
    )
    weights_out = lax.all_gather(attn_out, "view", axis=0, tiled=True)

    dma = pltpu.SemaphoreType.DMA
    vmem = pl.BlockSpec(memory_space=pltpu.VMEM)
    hbm = pl.BlockSpec(memory_space=pl.ANY)
    resid, mixed = pl.pallas_call(
        functools.partial(kernel, (V, R, H, g, T, rows, W, Wp, C, head)),
        out_shape=[jax.ShapeDtypeStruct((rows, W, C), BF16)] * 2,
        in_specs=[vmem, vmem, vmem, vmem, hbm, hbm],
        out_specs=[vmem, vmem],
        scratch_shapes=[
            pltpu.VMEM((R, 2, C), F32),
            pltpu.VMEM((R * B + 2 * Wp, C), BF16),
            pltpu.VMEM((9, C, Cr), BF16),
            pltpu.VMEM((3, M, Cr), F32),
            pltpu.VMEM((R * B, Cr), BF16),
            pltpu.VMEM((R, B, Cr), BF16),
            pltpu.VMEM((g, 3, C, C // V), BF16),
            pltpu.VMEM((g * T, C), BF16),
            pltpu.VMEM((H, g, T, C), BF16),
            pltpu.VMEM((3, V * T, width), F32),
            pltpu.VMEM((V, T, width), BF16),
            pltpu.VMEM((H, g * T, width), BF16),
            dma((2,)),
            dma((R,)),
            dma((R,)),
            dma((R,)),
            dma((R,)),
            dma((R,)),
            dma((R,)),
            dma((R,)),
            dma((R,)),
            dma((g,)),
            dma((g,)),
            dma((g,)),
            dma((g,)),
            dma((g,)),
            dma((g,)),
            dma((2, H, g)),
            dma((2, H, g)),
            dma((V,)),
            dma((V,)),
        ],
        compiler_params=pltpu.CompilerParams(
            collective_id=0, has_side_effects=True, vmem_limit_bytes=56 * 2**20
        ),
        cost_estimate=pl.CostEstimate(
            flops=2 * R * B * C * Cr * 9, bytes_accessed=40_000_000, transcendentals=0
        ),
    )(
        latent.reshape(rows, W, C),
        film,
        affine,
        scale,
        conv_w.reshape(9, C, Cr),
        attn_in,
    )
    projected = jnp.dot(
        mixed.reshape(rows * W, C), weights_out, preferred_element_type=F32
    ).reshape(rows, W, C)
    return (resid.astype(F32) + projected).astype(BF16).reshape(latent.shape)


def solution(mesh):
    placed = (
        P(None, "view", "row", None, None),
        P(),
        P(),
        P(None, "view"),
        P(),
        P(),
        P(),
        P(None, None, None, "row"),
        P(),
        P(),
        P(None, None, "view"),
        P("view", None),
        P(),
    )
    return jax.shard_map(
        local,
        mesh=mesh,
        in_specs=placed,
        out_specs=P(None, "view", "row", None, None),
        check_vma=False,
    )
```

```python
import functools
import math

import jax
import jax.numpy as jnp
from jax import lax
from jax.experimental import pallas as pl
from jax.experimental.pallas import tpu as pltpu
from jax.sharding import PartitionSpec as P

GROUPS = 32
EPS = 1e-05
F32 = jnp.float32
BF16 = jnp.bfloat16
HIGHEST = lax.Precision.HIGHEST


def up(n, m):
    return (n + m - 1) // m * m


def dot_t(a, b):
    return lax.dot_general(a, b, (((1,), (1,)), ((), ())), preferred_element_type=F32)


def one_hot(shape, long_axis, size):
    long = lax.broadcasted_iota(jnp.int32, shape, long_axis)
    short = lax.broadcasted_iota(jnp.int32, shape, 1 - long_axis) * size
    return (long >= short) & (long < short + size)


def kernel(
    dims,
    x_ref,
    film_ref,
    gn_gain_ref,
    gn_bias_ref,
    conv_bias_ref,
    ln_gain_ref,
    scale_ref,
    conv_hbm,
    attn_hbm,
    resid_ref,
    mixed_ref,
    stat,
    act,
    conv_w,
    acc,
    conv_s,
    conv_r,
    attn_w,
    ny,
    ally,
    qkv,
    mix_s,
    mix_r,
    load_sem,
    stat_ss,
    stat_rs,
    act_ss,
    act_rs,
    fwd_ss,
    fwd_rs,
    conv_ss,
    conv_rs,
    attn_ss,
    attn_rs,
    attn_fs,
    attn_fr,
    pair_ss,
    pair_rs,
    line_ss,
    line_rs,
    mix_ss,
    mix_rs,
):
    V, R, H, g, T, rows, W, Wp, C, head = dims
    B = rows * Wp
    Cr = conv_w.shape[1] // 3
    v = lax.axis_index("view")
    r = lax.axis_index("row")
    h = v % H
    q = v // H
    core = r % 2
    sib = r + 1 - 2 * core

    def at(view=None, row=None):
        return (v if view is None else view, r if row is None else row)

    def remote(src, dst, ss, rs, device):
        return pltpu.make_async_remote_copy(
            src_ref=src,
            dst_ref=dst,
            send_sem=ss,
            recv_sem=rs,
            device_id=device,
            device_id_type=pl.DeviceIdType.MESH,
        )

    load_conv = pltpu.make_async_copy(conv_hbm, conv_w, load_sem.at[0])
    load_conv.start()
    barrier = pltpu.get_barrier_semaphore()
    for o in range(1, R):
        pl.semaphore_signal(
            barrier, inc=1, device_id=at(row=(r + o) % R), device_id_type=pl.DeviceIdType.MESH
        )
    for o in range(1, V):
        pl.semaphore_signal(
            barrier, inc=1, device_id=at(view=(v + o) % V), device_id_type=pl.DeviceIdType.MESH
        )

    x = x_ref[...].astype(F32).reshape(rows * W, C)
    size = C // GROUPS
    into = one_hot((C, 128), 0, size).astype(F32)
    back = one_hot((128, C), 1, size).astype(F32)
    count = rows * W * size

    def spread(total):
        total = jnp.broadcast_to(total, (8, C))
        grouped = jnp.dot(total, into, precision=HIGHEST, preferred_element_type=F32)
        return jnp.dot(grouped, back, precision=HIGHEST, preferred_element_type=F32)[0:1]

    mean_here = spread(jnp.sum(x, axis=0, keepdims=True)) * (1.0 / count)
    off = x - mean_here
    square_here = spread(jnp.sum(off * off, axis=0, keepdims=True))
    stat[r, 0:1, :] = mean_here
    stat[r, 1:2, :] = square_here

    pl.semaphore_wait(barrier, R - 1 + V - 1)

    stat_copies = []
    for o in range(1, R):
        copy = remote(
            stat.at[r], stat.at[r], stat_ss.at[o], stat_rs.at[o], at(row=(r + o) % R)
        )
        copy.start()
        stat_copies.append(copy)

    half = C // 2
    Ca = attn_hbm.shape[1]
    mine = pl.ds(pl.multiple_of(core * half, half), half)

    def shard(k, columns):
        return attn_w.at[:, pl.ds(pl.multiple_of(k * Ca, 16), Ca), columns]

    def attn_send(k):
        return remote(
            attn_hbm.at[:, :, mine],
            shard(v % g, mine),
            attn_ss.at[k],
            attn_rs.at[v % g],
            at(view=v // g + H * k),
        )

    load_attn = pltpu.make_async_copy(attn_hbm, shard(v % g, slice(None)), load_sem.at[1])
    for k in range(g):
        here = v // g + H * k == v

        @pl.when(here)
        def _():
            load_attn.start()

        @pl.when(jnp.logical_not(here))
        def _():
            attn_send(k).start()

    for copy in stat_copies:
        copy.wait()
    means = [stat[d, 0:1, :] for d in range(R)]
    mean = sum(means[1:], means[0]) * (1.0 / R)
    total = jnp.zeros((1, C), F32)
    for d in range(R):
        gap = means[d] - mean
        total = total + stat[d, 1:2, :] + count * (gap * gap)
    rstd = lax.rsqrt(total * (1.0 / (count * R)) + EPS)
    film_gain = 1.0 + film_ref[:, :C]
    gain = rstd * (gn_gain_ref[...].reshape(1, C) * film_gain)
    shift = gn_bias_ref[...].reshape(1, C) * film_gain + film_ref[:, C:]
    hidden = (x - mean) * gain + shift
    hidden = hidden / (1.0 + jnp.exp(-hidden))

    def pad(values):
        parts = []
        for i in range(rows):
            parts.append(values[i * W : (i + 1) * W])
            parts.append(jnp.zeros((Wp - W, C), F32))
        return jnp.concatenate(parts, axis=0)

    def block(d):
        return act.at[pl.ds(pl.multiple_of(B * d, 16), B), :]

    act[pl.ds(pl.multiple_of(B * r, 16), B), :] = pad(hidden).astype(BF16)

    act_copies = []
    for o in range(1, R // 2):
        copy = remote(
            block(r), block(r), act_ss.at[o], act_rs.at[o], at(row=(r + 2 * o) % R)
        )
        copy.start()
        act_copies.append(copy)
    forwards = [remote(block(r), block(r), fwd_ss.at[0], fwd_rs.at[0], at(row=sib))]
    forwards[0].start()

    acc[...] = jnp.zeros(acc.shape, F32)

    def convolve(pair):
        start = pl.multiple_of(pair * 2 * B, 16)

        def taps(i, carry):
            lines = act[pl.ds(start, 2 * B), :]
            out = pl.ds(pl.multiple_of(start + (2 - i) * Wp, 16), 2 * B)
            acc[out, :] += dot_t(lines, conv_w[i])
            return carry

        lax.fori_loop(0, 3, taps, 0)

    load_conv.wait()
    forwards[0].wait_recv()
    convolve(r // 2)
    for o in range(1, R // 2):
        act_copies[o - 1].wait_recv()
        source = (r + R - 2 * o) % R
        copy = remote(
            block(source), block(source), fwd_ss.at[o], fwd_rs.at[o], at(row=sib)
        )
        copy.start()
        forwards.append(copy)
    for o in range(1, R // 2):
        forwards[o].wait_recv()
        convolve((r // 2 + R // 2 - o) % (R // 2))

    for copy in act_copies + forwards:
        copy.wait_send()

    def combine(d, carry):
        sums = acc[pl.ds(pl.multiple_of(B * d + Wp, 16), B), :]
        left = sums[:, :Cr]
        left = jnp.concatenate([left[B - 1 :], left[: B - 1]], axis=0)
        right = sums[:, 2 * Cr :]
        right = jnp.concatenate([right[1:], right[:1]], axis=0)
        sums = left + sums[:, Cr : 2 * Cr] + right
        conv_s[pl.ds(pl.multiple_of(B * d, 16), B), :] = sums.astype(BF16)
        return carry

    lax.fori_loop(0, R, combine, 0)

    conv_copies = []
    for o in range(1, R):
        to = (r + o) % R
        copy = remote(
            conv_s.at[pl.ds(pl.multiple_of(B * to, 16), B), :],
            conv_r.at[r],
            conv_ss.at[o],
            conv_rs.at[o],
            at(row=to),
        )
        copy.start()
        conv_copies.append(copy)
    conv_r[r] = conv_s[pl.ds(pl.multiple_of(B * r, 16), B), :]

    def attn_forward(k):
        part = shard(k, mine)
        return remote(part, part, attn_fs.at[k], attn_fr.at[k], at(row=sib))

    for k in range(g):

        @pl.when(g * h + k != v)
        def _():
            part = shard(k, mine)
            remote(
                part, part, attn_ss.at[k], attn_rs.at[k], at(view=(v + 1) % V)
            ).wait_recv()
            attn_forward(k).start()

    for copy in conv_copies:
        copy.wait()
    conv = jnp.concatenate([conv_r[d].astype(F32) for d in range(R)], axis=1)
    resid = (pad(x_ref[...].astype(F32).reshape(rows * W, C)) + conv + conv_bias_ref[...].reshape(1, C)).astype(
        BF16
    )
    for i in range(rows):
        resid_ref[i] = resid[i * Wp : i * Wp + W]
    resid = resid.astype(F32)
    middle = jnp.mean(resid, axis=1, keepdims=True)
    gap = resid - middle
    var = jnp.mean(gap * gap, axis=1, keepdims=True)
    ny[0:B, :] = (gap * lax.rsqrt(var + EPS) * ln_gain_ref[...].reshape(1, C)).astype(BF16)
    if g * T > B:
        ny[B : g * T, :] = jnp.zeros((g * T - B, C), BF16)

    def share(k):
        return pl.ds(pl.multiple_of(k * T, 16), T)

    def view_of(part, group):
        return part * H + group

    ally[q, h] = ny[share(q), :]
    pair_copies = []
    for o in range(1, g):
        to = (q + o) % g
        copy = remote(
            ny.at[share(to), :], ally.at[q, h], pair_ss.at[o], pair_rs.at[o], at(view=view_of(to, h))
        )
        copy.start()
        pair_copies.append(copy)

    beside = h + 1 - 2 * (h % 2)
    above = (h + 2) % H

    def hop(way, o):
        part = ally.at[(q + g - o) % g, above if way == 2 else h]
        return remote(
            part,
            part,
            line_ss.at[way, o],
            line_rs.at[way, o],
            at(view=view_of(q, above if way == 1 else beside)),
        )

    for o in range(g):
        if o > 0:
            pair_copies[o - 1].wait_recv()
        hop(1, o).start()
        hop(0, o).start()
        if o > 0:
            hop(1, o - 1).wait_recv()
            hop(2, o - 1).start()
    hop(1, g - 1).wait_recv()
    hop(2, g - 1).start()

    for k in range(g):
        here = v // g + H * k == v

        @pl.when(here)
        def _():
            load_attn.wait()

        @pl.when(jnp.logical_not(here))
        def _():
            attn_send(k).wait_send()

        @pl.when(g * h + k != v)
        def _():
            attn_forward(k).wait()

    for copy in pair_copies:
        copy.wait_send()
    for o in range(g):
        hop(0, o).wait()
        hop(1, o).wait_send()
        hop(2, o).wait()

    width = qkv.shape[-1]
    everything = ally[...].reshape(V * T, C)
    for kind in range(3):
        qkv[kind] = dot_t(everything, attn_w[kind]).astype(BF16).astype(F32)

    into_heads = one_hot((width, 128), 0, head).astype(BF16)
    from_heads = one_hot((128, width), 1, head).astype(BF16)
    lane = lax.broadcasted_iota(jnp.int32, (1, 128), 1)
    scale = jnp.zeros((1, 128), F32)
    for k in range(width // head):
        scale = jnp.where(lane == k, scale_ref[h * (width // head) + k], scale)
    scale = scale * (1.0 / math.sqrt(head))

    def attend(k, carry):
        u = (v + 1 + k) % V
        query = qkv[0, pl.ds(pl.multiple_of(u * T, 16), T), :]
        product = (query[None] * qkv[1].reshape(V, T, width)).reshape(V * T, width)
        top = product.astype(BF16)
        low = (product - top.astype(F32)).astype(BF16)
        scores = jnp.dot(top, into_heads, preferred_element_type=F32) + jnp.dot(
            low, into_heads, preferred_element_type=F32
        )
        scores = (scores * scale).reshape(V, T, 128)
        weights = jnp.exp(scores - jnp.max(scores, axis=0, keepdims=True))
        weights = weights / jnp.sum(weights, axis=0, keepdims=True)
        weights = jnp.dot(
            weights.reshape(V * T, 128).astype(BF16), from_heads, preferred_element_type=F32
        )
        mixed = jnp.sum((weights * qkv[2]).reshape(V, T, width), axis=0).astype(BF16)

        @pl.when(u == v)
        def _():
            mix_r[h, share(q), :] = mixed

        @pl.when(u != v)
        def _():
            mix_s[u] = mixed
            remote(
                mix_s.at[u],
                mix_r.at[h, share(q), :],
                mix_ss.at[u],
                mix_rs.at[v],
                at(view=u),
            ).start()

        return carry

    lax.fori_loop(0, V, attend, 0)

    def finish(k, carry):
        u = (v + 1 + k) % V
        remote(
            mix_s.at[u],
            mix_r.at[u % H, share(u // H), :],
            mix_ss.at[u],
            mix_rs.at[u],
            at(view=u),
        ).wait()
        return carry

    lax.fori_loop(0, V - 1, finish, 0)
    mixed = jnp.concatenate([mix_r[k].astype(F32) for k in range(H)], axis=1).astype(BF16)
    for i in range(rows):
        mixed_ref[i] = mixed[i * Wp : i * Wp + W]


def local(
    latent,
    gn_gain,
    gn_bias,
    cam_idx,
    noise_idx,
    cam_table,
    noise_table,
    conv_w,
    conv_bias,
    ln_gain,
    attn_in,
    attn_out,
    head_scale,
):
    _, _, rows, W, C = latent.shape
    V = lax.axis_size("view")
    R = lax.axis_size("row")
    heads = head_scale.shape[0]
    head = C // heads
    H = math.gcd(V, heads)
    g = V // H
    Wp = up(W + 1, 16)
    B = rows * Wp
    T = up(-(-B // g), 16)
    Cr = conv_w.shape[-1]
    width = C // H

    film = lax.dynamic_slice_in_dim(
        cam_table, cam_idx[0, 0], 1, 0, allow_negative_indices=False
    ).astype(F32) + lax.dynamic_slice_in_dim(
        noise_table, noise_idx[0], 1, 0, allow_negative_indices=False
    ).astype(F32)
    weights_out = lax.all_gather(attn_out, "view", axis=0, tiled=True)

    dma = pltpu.SemaphoreType.DMA
    vmem = pl.BlockSpec(memory_space=pltpu.VMEM)
    smem = pl.BlockSpec(memory_space=pltpu.SMEM)
    hbm = pl.BlockSpec(memory_space=pl.ANY)
    resid, mixed = pl.pallas_call(
        functools.partial(kernel, (V, R, H, g, T, rows, W, Wp, C, head)),
        out_shape=[jax.ShapeDtypeStruct((rows, W, C), BF16)] * 2,
        in_specs=[vmem] * 6 + [smem] + [hbm, hbm],
        out_specs=[vmem, vmem],
        scratch_shapes=[
            pltpu.VMEM((R, 2, C), F32),
            pltpu.VMEM((R * B, C), BF16),
            pltpu.VMEM((3, 3 * Cr, C), BF16),
            pltpu.VMEM((R * B + 2 * Wp, 3 * Cr), F32),
            pltpu.VMEM((R * B, Cr), BF16),
            pltpu.VMEM((R, B, Cr), BF16),
            pltpu.VMEM((3, C // H, C), BF16),
            pltpu.VMEM((g * T, C), BF16),
            pltpu.VMEM((g, H, T, C), BF16),
            pltpu.VMEM((3, V * T, width), F32),
            pltpu.VMEM((V, T, width), BF16),
            pltpu.VMEM((H, g * T, width), BF16),
            dma((2,)),
            dma((R,)),
            dma((R,)),
            dma((R,)),
            dma((R,)),
            dma((R,)),
            dma((R,)),
            dma((R,)),
            dma((R,)),
            dma((g,)),
            dma((g,)),
            dma((g,)),
            dma((g,)),
            dma((g,)),
            dma((g,)),
            dma((3, g)),
            dma((3, g)),
            dma((V,)),
            dma((V,)),
        ],
        compiler_params=pltpu.CompilerParams(
            collective_id=0, has_side_effects=True, vmem_limit_bytes=56 * 2**20
        ),
        cost_estimate=pl.CostEstimate(
            flops=2 * R * B * C * Cr * 9, bytes_accessed=40_000_000, transcendentals=0
        ),
    )(
        latent.reshape(rows, W, C),
        film,
        gn_gain,
        gn_bias,
        conv_bias,
        ln_gain,
        head_scale,
        jnp.swapaxes(conv_w, 2, 3).reshape(3, 3 * Cr, C),
        jnp.swapaxes(attn_in, 1, 2),
    )
    projected = jnp.dot(
        mixed.reshape(rows * W, C), weights_out, preferred_element_type=F32
    ).reshape(rows, W, C)
    return (resid.astype(F32) + projected).astype(BF16).reshape(latent.shape)


def solution(mesh):
    placed = (
        P(None, "view", "row", None, None),
        P(),
        P(),
        P(None, "view"),
        P(),
        P(),
        P(),
        P(None, None, None, "row"),
        P(),
        P(),
        P(None, None, "view"),
        P("view", None),
        P(),
    )
    return jax.shard_map(
        local,
        mesh=mesh,
        in_specs=placed,
        out_specs=P(None, "view", "row", None, None),
        check_vma=False,
    )
```

```python
import functools
import math

import jax
import jax.numpy as jnp
from jax import lax
from jax.experimental import pallas as pl
from jax.experimental.pallas import tpu as pltpu
from jax.sharding import PartitionSpec as P

GROUPS = 32
EPS = 1e-05
F32 = jnp.float32
BF16 = jnp.bfloat16


def up(n, m):
    return (n + m - 1) // m * m


def dot_t(a, b):
    return lax.dot_general(a, b, (((1,), (1,)), ((), ())), preferred_element_type=F32)


def one_hot(shape, long_axis, size):
    long = lax.broadcasted_iota(jnp.int32, shape, long_axis)
    short = lax.broadcasted_iota(jnp.int32, shape, 1 - long_axis) * size
    return (long >= short) & (long < short + size)


def kernel(
    dims,
    x_ref,
    film_ref,
    gn_gain_ref,
    gn_bias_ref,
    conv_bias_ref,
    ln_gain_ref,
    scale_ref,
    conv_hbm,
    attn_hbm,
    proj_hbm,
    out_ref,
    stat,
    act,
    conv_w,
    acc,
    conv_s,
    conv_r,
    attn_w,
    proj_w,
    ny,
    ally,
    qkv,
    mix_s,
    mix_r,
    load_sem,
    stat_ss,
    stat_rs,
    act_ss,
    act_rs,
    fwd_ss,
    fwd_rs,
    conv_ss,
    conv_rs,
    attn_ss,
    attn_rs,
    attn_fs,
    attn_fr,
    pair_ss,
    pair_rs,
    line_ss,
    line_rs,
    mix_ss,
    mix_rs,
    cross_ss,
    cross_rs,
    proj_ss,
    proj_rs,
    proj_fs,
    proj_fr,
):
    V, R, H, g, T, rows, W, Wp, C, head = dims
    B = rows * Wp
    Cr = conv_w.shape[1] // 3
    v = lax.axis_index("view")
    r = lax.axis_index("row")
    h = v % H
    q = v // H
    core = r % 2
    sib = r + 1 - 2 * core

    def at(view=None, row=None):
        return (v if view is None else view, r if row is None else row)

    def remote(src, dst, ss, rs, device):
        return pltpu.make_async_remote_copy(
            src_ref=src,
            dst_ref=dst,
            send_sem=ss,
            recv_sem=rs,
            device_id=device,
            device_id_type=pl.DeviceIdType.MESH,
        )

    load_conv = pltpu.make_async_copy(conv_hbm, conv_w, load_sem.at[0])
    Ca = proj_hbm.shape[0]
    half = C // 2
    mine = pl.ds(pl.multiple_of(core * half, half), half)

    def proj_block(view, columns):
        return proj_w.at[pl.ds(pl.multiple_of(view * Ca, 16), Ca), columns]

    load_proj = pltpu.make_async_copy(proj_hbm, proj_block(v, slice(None)), load_sem.at[2])
    load_proj.start()
    load_conv.start()
    barrier = pltpu.get_barrier_semaphore()
    for o in range(1, R):
        pl.semaphore_signal(
            barrier, inc=1, device_id=at(row=(r + o) % R), device_id_type=pl.DeviceIdType.MESH
        )
    for o in range(1, V):
        pl.semaphore_signal(
            barrier, inc=1, device_id=at(view=(v + o) % V), device_id_type=pl.DeviceIdType.MESH
        )

    x = x_ref[...].astype(F32).reshape(rows * W, C)
    size = C // GROUPS
    into = one_hot((C, 128), 0, size).astype(F32).astype(BF16)
    back = one_hot((128, C), 1, size).astype(F32).astype(BF16)
    count = rows * W * size

    def sum_dot(values, ones):
        line = lax.broadcasted_iota(jnp.int32, (8, values.shape[1]), 0)
        values = jnp.broadcast_to(values, line.shape)
        top = values.astype(BF16).astype(F32)
        rest = values - top
        middle = rest.astype(BF16).astype(F32)
        low = rest - middle
        pieces = jnp.where(line == 0, top, jnp.where(line == 1, middle, low))
        pieces = jnp.where(line < 3, pieces, 0.0).astype(BF16)
        return jnp.sum(
            jnp.dot(pieces, ones, preferred_element_type=F32), axis=0, keepdims=True
        )

    def spread(total):
        return sum_dot(sum_dot(total, into), back)

    mean_here = spread(jnp.sum(x, axis=0, keepdims=True)) * (1.0 / count)
    off = x - mean_here
    square_here = spread(jnp.sum(off * off, axis=0, keepdims=True))
    stat[r, 0:1, :] = mean_here
    stat[r, 1:2, :] = square_here

    pl.semaphore_wait(barrier, R - 1 + V - 1)

    stat_copies = []
    for o in range(1, R):
        copy = remote(
            stat.at[r], stat.at[r], stat_ss.at[o], stat_rs.at[o], at(row=(r + o) % R)
        )
        copy.start()
        stat_copies.append(copy)

    beside = h + 1 - 2 * (h % 2)
    above = (h + 2) % H

    def view_of(part, group):
        return part * H + group

    def hop(slot, ss, rs, way, o):
        part = slot((q + g - o) % g, above if way == 2 else h)
        return remote(
            part,
            part,
            ss.at[way, o],
            rs.at[way, o],
            at(view=view_of(q, above if way == 1 else beside)),
        )

    def proj_slot(part, group):
        return proj_block(view_of(part, group), mine)

    proj_hop = functools.partial(hop, proj_slot, proj_ss, proj_rs)
    load_proj.wait()
    proj_hop(1, 0).start()
    proj_hop(0, 0).start()
    cross_copies = []
    for o in range(1, g):
        copy = remote(
            proj_slot(q, h),
            proj_slot(q, h),
            cross_ss.at[o],
            cross_rs.at[o],
            at(view=view_of((q + o) % g, h)),
        )
        copy.start()
        cross_copies.append(copy)

    def shard(k, columns):
        return attn_w.at[:, pl.ds(pl.multiple_of(k * Ca, 16), Ca), columns]

    def attn_send(k):
        return remote(
            attn_hbm.at[:, :, mine],
            shard(v % g, mine),
            attn_ss.at[k],
            attn_rs.at[v % g],
            at(view=v // g + H * k),
        )

    load_attn = pltpu.make_async_copy(attn_hbm, shard(v % g, slice(None)), load_sem.at[1])
    for k in range(g):
        here = v // g + H * k == v

        @pl.when(here)
        def _():
            load_attn.start()

        @pl.when(jnp.logical_not(here))
        def _():
            attn_send(k).start()

    for copy in stat_copies:
        copy.wait()
    means = [stat[d, 0:1, :] for d in range(R)]
    mean = sum(means[1:], means[0]) * (1.0 / R)
    total = jnp.zeros((1, C), F32)
    for d in range(R):
        gap = means[d] - mean
        total = total + stat[d, 1:2, :] + count * (gap * gap)
    rstd = lax.rsqrt(total * (1.0 / (count * R)) + EPS)
    film_gain = 1.0 + film_ref[:, :C]
    gain = rstd * (gn_gain_ref[...].reshape(1, C) * film_gain)
    shift = gn_bias_ref[...].reshape(1, C) * film_gain + film_ref[:, C:]
    hidden = (x - mean) * gain + shift
    hidden = hidden / (1.0 + jnp.exp(-hidden))

    def pad(values):
        parts = []
        for i in range(rows):
            parts.append(values[i * W : (i + 1) * W])
            parts.append(jnp.zeros((Wp - W, C), F32))
        return jnp.concatenate(parts, axis=0)

    def block(d):
        return act.at[pl.ds(pl.multiple_of(B * d, 16), B), :]

    act[pl.ds(pl.multiple_of(B * r, 16), B), :] = pad(hidden).astype(BF16)

    act_copies = []
    for o in range(1, R // 2):
        copy = remote(
            block(r), block(r), act_ss.at[o], act_rs.at[o], at(row=(r + 2 * o) % R)
        )
        copy.start()
        act_copies.append(copy)
    forwards = [remote(block(r), block(r), fwd_ss.at[0], fwd_rs.at[0], at(row=sib))]
    forwards[0].start()

    acc[...] = jnp.zeros(acc.shape, F32)

    def convolve(pair):
        start = pl.multiple_of(pair * 2 * B, 16)

        def taps(i, carry):
            lines = act[pl.ds(start, 2 * B), :]
            out = pl.ds(pl.multiple_of(start + (2 - i) * Wp, 16), 2 * B)
            acc[out, :] += dot_t(lines, conv_w[i])
            return carry

        lax.fori_loop(0, 3, taps, 0)

    load_conv.wait()
    forwards[0].wait_recv()
    convolve(r // 2)
    for o in range(1, R // 2):
        act_copies[o - 1].wait_recv()
        source = (r + R - 2 * o) % R
        copy = remote(
            block(source), block(source), fwd_ss.at[o], fwd_rs.at[o], at(row=sib)
        )
        copy.start()
        forwards.append(copy)
    for o in range(1, R // 2):
        forwards[o].wait_recv()
        convolve((r // 2 + R // 2 - o) % (R // 2))

    for copy in act_copies + forwards:
        copy.wait_send()

    for o in range(1, g):
        cross_copies[o - 1].wait()
        proj_hop(1, o).start()
        proj_hop(0, o).start()
    for o in range(g):
        proj_hop(1, o).wait_recv()
        proj_hop(2, o).start()

    def combine(d, carry):
        sums = acc[pl.ds(pl.multiple_of(B * d + Wp, 16), B), :]
        left = sums[:, :Cr]
        left = jnp.concatenate([left[B - 1 :], left[: B - 1]], axis=0)
        right = sums[:, 2 * Cr :]
        right = jnp.concatenate([right[1:], right[:1]], axis=0)
        sums = left + sums[:, Cr : 2 * Cr] + right
        conv_s[pl.ds(pl.multiple_of(B * d, 16), B), :] = sums.astype(BF16)
        return carry

    lax.fori_loop(0, R, combine, 0)

    conv_copies = []
    for o in range(1, R):
        to = (r + o) % R
        copy = remote(
            conv_s.at[pl.ds(pl.multiple_of(B * to, 16), B), :],
            conv_r.at[r],
            conv_ss.at[o],
            conv_rs.at[o],
            at(row=to),
        )
        copy.start()
        conv_copies.append(copy)
    conv_r[r] = conv_s[pl.ds(pl.multiple_of(B * r, 16), B), :]

    def attn_forward(k):
        part = shard(k, mine)
        return remote(part, part, attn_fs.at[k], attn_fr.at[k], at(row=sib))

    for k in range(g):

        @pl.when(g * h + k != v)
        def _():
            part = shard(k, mine)
            remote(
                part, part, attn_ss.at[k], attn_rs.at[k], at(view=(v + 1) % V)
            ).wait_recv()
            attn_forward(k).start()

    for copy in conv_copies:
        copy.wait()
    conv = jnp.concatenate([conv_r[d].astype(F32) for d in range(R)], axis=1)
    resid = (pad(x_ref[...].astype(F32).reshape(rows * W, C)) + conv + conv_bias_ref[...].reshape(1, C)).astype(
        BF16
    )
    for i in range(rows):
        out_ref[i] = resid[i * Wp : i * Wp + W]
    resid = resid.astype(F32)
    middle = jnp.mean(resid, axis=1, keepdims=True)
    gap = resid - middle
    var = jnp.mean(gap * gap, axis=1, keepdims=True)
    ny[0:B, :] = (gap * lax.rsqrt(var + EPS) * ln_gain_ref[...].reshape(1, C)).astype(BF16)
    if g * T > B:
        ny[B : g * T, :] = jnp.zeros((g * T - B, C), BF16)

    def share(k):
        return pl.ds(pl.multiple_of(k * T, 16), T)

    ally[q, h] = ny[share(q), :]
    pair_copies = []
    for o in range(1, g):
        to = (q + o) % g
        copy = remote(
            ny.at[share(to), :], ally.at[q, h], pair_ss.at[o], pair_rs.at[o], at(view=view_of(to, h))
        )
        copy.start()
        pair_copies.append(copy)

    line_hop = functools.partial(hop, lambda part, group: ally.at[part, group], line_ss, line_rs)
    for o in range(g):
        if o > 0:
            pair_copies[o - 1].wait_recv()
        line_hop(1, o).start()
        line_hop(0, o).start()
        if o > 0:
            line_hop(1, o - 1).wait_recv()
            line_hop(2, o - 1).start()
    line_hop(1, g - 1).wait_recv()
    line_hop(2, g - 1).start()

    for k in range(g):
        here = v // g + H * k == v

        @pl.when(here)
        def _():
            load_attn.wait()

        @pl.when(jnp.logical_not(here))
        def _():
            attn_send(k).wait_send()

        @pl.when(g * h + k != v)
        def _():
            attn_forward(k).wait()

    for copy in pair_copies:
        copy.wait_send()
    for o in range(g):
        line_hop(0, o).wait()
        line_hop(1, o).wait_send()
        line_hop(2, o).wait()

    width = qkv.shape[-1]
    everything = ally[...].reshape(V * T, C)
    for kind in range(3):
        qkv[kind] = dot_t(everything, attn_w[kind]).astype(BF16).astype(F32)

    proj_forwards = []
    for o in range(g):
        proj_hop(0, o).wait()
        proj_hop(1, o).wait_send()
        proj_hop(2, o).wait()
    for o in range(1, V):
        part = proj_block((v + o) % V, mine)
        copy = remote(part, part, proj_fs.at[o], proj_fr.at[o], at(row=sib))
        copy.start()
        proj_forwards.append(copy)

    into_heads = one_hot((width, 128), 0, head).astype(BF16)
    from_heads = one_hot((128, width), 1, head).astype(BF16)
    lane = lax.broadcasted_iota(jnp.int32, (1, 128), 1)
    scale = jnp.zeros((1, 128), F32)
    for k in range(width // head):
        scale = jnp.where(lane == k, scale_ref[h * (width // head) + k], scale)
    scale = scale * (1.0 / math.sqrt(head))

    def attend(k, carry):
        u = (v + 1 + k) % V
        query = qkv[0, pl.ds(pl.multiple_of(u * T, 16), T), :]
        product = (query[None] * qkv[1].reshape(V, T, width)).reshape(V * T, width)
        top = product.astype(BF16)
        low = (product - top.astype(F32)).astype(BF16)
        scores = jnp.dot(top, into_heads, preferred_element_type=F32) + jnp.dot(
            low, into_heads, preferred_element_type=F32
        )
        scores = (scores * scale).reshape(V, T, 128)
        weights = jnp.exp(scores - jnp.max(scores, axis=0, keepdims=True))
        weights = weights / jnp.sum(weights, axis=0, keepdims=True)
        weights = jnp.dot(
            weights.reshape(V * T, 128).astype(BF16), from_heads, preferred_element_type=F32
        )
        mixed = jnp.sum((weights * qkv[2]).reshape(V, T, width), axis=0).astype(BF16)

        @pl.when(u == v)
        def _():
            mix_r[h, share(q), :] = mixed

        @pl.when(u != v)
        def _():
            mix_s[u] = mixed
            remote(
                mix_s.at[u],
                mix_r.at[h, share(q), :],
                mix_ss.at[u],
                mix_rs.at[v],
                at(view=u),
            ).start()

        return carry

    lax.fori_loop(0, V, attend, 0)

    def finish(k, carry):
        u = (v + 1 + k) % V
        remote(
            mix_s.at[u],
            mix_r.at[u % H, share(u // H), :],
            mix_ss.at[u],
            mix_rs.at[u],
            at(view=u),
        ).wait()
        return carry

    lax.fori_loop(0, V - 1, finish, 0)
    for copy in proj_forwards:
        copy.wait()
    mixed = jnp.concatenate([mix_r[k].astype(F32) for k in range(H)], axis=1).astype(BF16)
    projected = jnp.dot(mixed[:B], proj_w[...], preferred_element_type=F32)
    for i in range(rows):
        out_ref[i] = (out_ref[i].astype(F32) + projected[i * Wp : i * Wp + W]).astype(BF16)


def local(
    latent,
    gn_gain,
    gn_bias,
    cam_idx,
    noise_idx,
    cam_table,
    noise_table,
    conv_w,
    conv_bias,
    ln_gain,
    attn_in,
    attn_out,
    head_scale,
):
    _, _, rows, W, C = latent.shape
    V = lax.axis_size("view")
    R = lax.axis_size("row")
    heads = head_scale.shape[0]
    head = C // heads
    H = math.gcd(V, heads)
    g = V // H
    Wp = up(W + 1, 16)
    B = rows * Wp
    T = up(-(-B // g), 16)
    Cr = conv_w.shape[-1]
    width = C // H

    film = lax.dynamic_slice_in_dim(
        cam_table, cam_idx[0, 0], 1, 0, allow_negative_indices=False
    ).astype(F32) + lax.dynamic_slice_in_dim(
        noise_table, noise_idx[0], 1, 0, allow_negative_indices=False
    ).astype(F32)

    dma = pltpu.SemaphoreType.DMA
    vmem = pl.BlockSpec(memory_space=pltpu.VMEM)
    smem = pl.BlockSpec(memory_space=pltpu.SMEM)
    hbm = pl.BlockSpec(memory_space=pl.ANY)
    out = pl.pallas_call(
        functools.partial(kernel, (V, R, H, g, T, rows, W, Wp, C, head)),
        out_shape=jax.ShapeDtypeStruct((rows, W, C), BF16),
        in_specs=[vmem] * 6 + [smem] + [hbm] * 3,
        out_specs=vmem,
        scratch_shapes=[
            pltpu.VMEM((R, 2, C), F32),
            pltpu.VMEM((R * B, C), BF16),
            pltpu.VMEM((3, 3 * Cr, C), BF16),
            pltpu.VMEM((R * B + 2 * Wp, 3 * Cr), F32),
            pltpu.VMEM((R * B, Cr), BF16),
            pltpu.VMEM((R, B, Cr), BF16),
            pltpu.VMEM((3, C // H, C), BF16),
            pltpu.VMEM((C, C), BF16),
            pltpu.VMEM((g * T, C), BF16),
            pltpu.VMEM((g, H, T, C), BF16),
            pltpu.VMEM((3, V * T, width), F32),
            pltpu.VMEM((V, T, width), BF16),
            pltpu.VMEM((H, g * T, width), BF16),
            dma((3,)),
            dma((R,)),
            dma((R,)),
            dma((R,)),
            dma((R,)),
            dma((R,)),
            dma((R,)),
            dma((R,)),
            dma((R,)),
            dma((g,)),
            dma((g,)),
            dma((g,)),
            dma((g,)),
            dma((g,)),
            dma((g,)),
            dma((3, g)),
            dma((3, g)),
            dma((V,)),
            dma((V,)),
            dma((g,)),
            dma((g,)),
            dma((3, g)),
            dma((3, g)),
            dma((V,)),
            dma((V,)),
        ],
        compiler_params=pltpu.CompilerParams(
            collective_id=0, has_side_effects=True, vmem_limit_bytes=56 * 2**20
        ),
        cost_estimate=pl.CostEstimate(
            flops=2 * R * B * C * Cr * 9, bytes_accessed=40_000_000, transcendentals=0
        ),
    )(
        latent.reshape(rows, W, C),
        film,
        gn_gain,
        gn_bias,
        conv_bias,
        ln_gain,
        head_scale,
        jnp.swapaxes(conv_w, 2, 3).reshape(3, 3 * Cr, C),
        jnp.swapaxes(attn_in, 1, 2),
        attn_out,
    )
    return out.reshape(latent.shape)


def solution(mesh):
    placed = (
        P(None, "view", "row", None, None),
        P(),
        P(),
        P(None, "view"),
        P(),
        P(),
        P(),
        P(None, None, None, "row"),
        P(),
        P(),
        P(None, None, "view"),
        P("view", None),
        P(),
    )
    return jax.shard_map(
        local,
        mesh=mesh,
        in_specs=placed,
        out_specs=P(None, "view", "row", None, None),
        check_vma=False,
    )
```

```python
import functools
import math

import jax
import jax.numpy as jnp
from jax import lax
from jax.experimental import pallas as pl
from jax.experimental.pallas import tpu as pltpu
from jax.sharding import PartitionSpec as P

GROUPS = 32
EPS = 1e-05
F32 = jnp.float32
BF16 = jnp.bfloat16


def up(n, m):
    return (n + m - 1) // m * m


def dot_t(a, b):
    return lax.dot_general(a, b, (((1,), (1,)), ((), ())), preferred_element_type=F32)


def one_hot(shape, long_axis, size):
    long = lax.broadcasted_iota(jnp.int32, shape, long_axis)
    short = lax.broadcasted_iota(jnp.int32, shape, 1 - long_axis) * size
    return (long >= short) & (long < short + size)


def kernel(
    dims,
    x_ref,
    film_ref,
    gn_gain_ref,
    gn_bias_ref,
    conv_bias_ref,
    ln_gain_ref,
    scale_ref,
    conv_hbm,
    attn_hbm,
    proj_hbm,
    out_ref,
    stat,
    act,
    conv_w,
    acc,
    conv_s,
    conv_r,
    attn_w,
    proj_w,
    ny,
    ally,
    qkv,
    mix_s,
    mix_r,
    load_sem,
    stat_ss,
    stat_rs,
    act_ss,
    act_rs,
    fwd_ss,
    fwd_rs,
    conv_ss,
    conv_rs,
    attn_ss,
    attn_rs,
    attn_fs,
    attn_fr,
    pair_ss,
    pair_rs,
    line_ss,
    line_rs,
    mix_ss,
    mix_rs,
    cross_ss,
    cross_rs,
    proj_ss,
    proj_rs,
    proj_fs,
    proj_fr,
    attn_xs,
    attn_xr,
    proj_xs,
    proj_xr,
):
    V, R, H, g, T, rows, W, Wp, C, head = dims
    B = rows * Wp
    Cr = conv_w.shape[1] // 3
    v = lax.axis_index("view")
    r = lax.axis_index("row")
    h = v % H
    q = v // H
    core = r % 2
    sib = r + 1 - 2 * core

    def at(view=None, row=None):
        return (v if view is None else view, r if row is None else row)

    def remote(src, dst, ss, rs, device):
        return pltpu.make_async_remote_copy(
            src_ref=src,
            dst_ref=dst,
            send_sem=ss,
            recv_sem=rs,
            device_id=device,
            device_id_type=pl.DeviceIdType.MESH,
        )

    load_conv = pltpu.make_async_copy(conv_hbm, conv_w, load_sem.at[0])
    Ca = proj_hbm.shape[0]
    half = C // 2
    mine = pl.ds(pl.multiple_of(core * half, half), half)

    nx = 2 if R == 4 and Ca % 32 == 0 else 1
    Cq = Ca // nx
    first = (r // 2) % nx * Cq
    across = (r + 2) % R

    def proj_block(view, columns):
        return proj_w.at[pl.ds(pl.multiple_of(view * Ca, 16), Ca), columns]

    def proj_quarter(view):
        return proj_w.at[pl.ds(pl.multiple_of(view * Ca + first, 16), Cq), mine]

    load_proj = pltpu.make_async_copy(proj_hbm, proj_block(v, slice(None)), load_sem.at[2])
    load_proj.start()
    load_conv.start()
    barrier = pltpu.get_barrier_semaphore()
    for o in range(1, R):
        pl.semaphore_signal(
            barrier, inc=1, device_id=at(row=(r + o) % R), device_id_type=pl.DeviceIdType.MESH
        )
    for o in range(1, V):
        pl.semaphore_signal(
            barrier, inc=1, device_id=at(view=(v + o) % V), device_id_type=pl.DeviceIdType.MESH
        )

    x = x_ref[...].astype(F32).reshape(rows * W, C)
    size = C // GROUPS
    into = one_hot((C, 128), 0, size).astype(F32).astype(BF16)
    back = one_hot((128, C), 1, size).astype(F32).astype(BF16)
    count = rows * W * size

    def sum_dot(values, ones):
        line = lax.broadcasted_iota(jnp.int32, (8, values.shape[1]), 0)
        values = jnp.broadcast_to(values, line.shape)
        top = values.astype(BF16).astype(F32)
        rest = values - top
        middle = rest.astype(BF16).astype(F32)
        low = rest - middle
        pieces = jnp.where(line == 0, top, jnp.where(line == 1, middle, low))
        pieces = jnp.where(line < 3, pieces, 0.0).astype(BF16)
        return jnp.sum(
            jnp.dot(pieces, ones, preferred_element_type=F32), axis=0, keepdims=True
        )

    def spread(total):
        return sum_dot(sum_dot(total, into), back)

    mean_here = spread(jnp.sum(x, axis=0, keepdims=True)) * (1.0 / count)
    off = x - mean_here
    square_here = spread(jnp.sum(off * off, axis=0, keepdims=True))
    stat[r, 0:1, :] = mean_here
    stat[r, 1:2, :] = square_here

    pl.semaphore_wait(barrier, R - 1 + V - 1)

    stat_copies = []
    for o in range(1, R):
        copy = remote(
            stat.at[r], stat.at[r], stat_ss.at[o], stat_rs.at[o], at(row=(r + o) % R)
        )
        copy.start()
        stat_copies.append(copy)

    beside = h + 1 - 2 * (h % 2)
    above = (h + 2) % H

    def view_of(part, group):
        return part * H + group

    def hop(slot, ss, rs, way, o):
        part = slot((q + g - o) % g, above if way == 2 else h)
        return remote(
            part,
            part,
            ss.at[way, o],
            rs.at[way, o],
            at(view=view_of(q, above if way == 1 else beside)),
        )

    def proj_slot(part, group):
        return proj_quarter(view_of(part, group))

    proj_hop = functools.partial(hop, proj_slot, proj_ss, proj_rs)
    load_proj.wait()
    proj_hop(1, 0).start()
    proj_hop(0, 0).start()
    cross_copies = []
    for o in range(1, g):
        copy = remote(
            proj_slot(q, h),
            proj_slot(q, h),
            cross_ss.at[o],
            cross_rs.at[o],
            at(view=view_of((q + o) % g, h)),
        )
        copy.start()
        cross_copies.append(copy)

    def shard(k, columns):
        return attn_w.at[:, pl.ds(pl.multiple_of(k * Ca, 16), Ca), columns]

    def attn_quarter(k):
        return attn_w.at[:, pl.ds(pl.multiple_of(k * Ca + first, 16), Cq), mine]

    def attn_send(k):
        return remote(
            attn_hbm.at[:, pl.ds(pl.multiple_of(first, 16), Cq), mine],
            attn_quarter(v % g),
            attn_ss.at[k],
            attn_rs.at[v % g],
            at(view=v // g + H * k),
        )

    load_attn = pltpu.make_async_copy(attn_hbm, shard(v % g, slice(None)), load_sem.at[1])
    for k in range(g):
        here = v // g + H * k == v

        @pl.when(here)
        def _():
            load_attn.start()

        @pl.when(jnp.logical_not(here))
        def _():
            attn_send(k).start()

    for copy in stat_copies:
        copy.wait()
    means = [stat[d, 0:1, :] for d in range(R)]
    mean = sum(means[1:], means[0]) * (1.0 / R)
    total = jnp.zeros((1, C), F32)
    for d in range(R):
        gap = means[d] - mean
        total = total + stat[d, 1:2, :] + count * (gap * gap)
    rstd = lax.rsqrt(total * (1.0 / (count * R)) + EPS)
    film_gain = 1.0 + film_ref[:, :C]
    gain = rstd * (gn_gain_ref[...].reshape(1, C) * film_gain)
    shift = gn_bias_ref[...].reshape(1, C) * film_gain + film_ref[:, C:]
    hidden = (x - mean) * gain + shift
    hidden = hidden / (1.0 + jnp.exp(-hidden))

    def pad(values):
        parts = []
        for i in range(rows):
            parts.append(values[i * W : (i + 1) * W])
            parts.append(jnp.zeros((Wp - W, C), F32))
        return jnp.concatenate(parts, axis=0)

    def block(d):
        return act.at[pl.ds(pl.multiple_of(B * d, 16), B), :]

    act[pl.ds(pl.multiple_of(B * r, 16), B), :] = pad(hidden).astype(BF16)

    act_copies = []
    for o in range(1, R // 2):
        copy = remote(
            block(r), block(r), act_ss.at[o], act_rs.at[o], at(row=(r + 2 * o) % R)
        )
        copy.start()
        act_copies.append(copy)
    forwards = [remote(block(r), block(r), fwd_ss.at[0], fwd_rs.at[0], at(row=sib))]
    forwards[0].start()

    acc[...] = jnp.zeros(acc.shape, F32)

    def convolve(pair):
        start = pl.multiple_of(pair * 2 * B, 16)

        def taps(i, carry):
            lines = act[pl.ds(start, 2 * B), :]
            out = pl.ds(pl.multiple_of(start + (2 - i) * Wp, 16), 2 * B)
            acc[out, :] += dot_t(lines, conv_w[i])
            return carry

        lax.fori_loop(0, 3, taps, 0)

    load_conv.wait()
    forwards[0].wait_recv()
    convolve(r // 2)
    for o in range(1, R // 2):
        act_copies[o - 1].wait_recv()
        source = (r + R - 2 * o) % R
        copy = remote(
            block(source), block(source), fwd_ss.at[o], fwd_rs.at[o], at(row=sib)
        )
        copy.start()
        forwards.append(copy)
    for o in range(1, R // 2):
        forwards[o].wait_recv()
        convolve((r // 2 + R // 2 - o) % (R // 2))

    for copy in act_copies + forwards:
        copy.wait_send()

    def combine(d, carry):
        sums = acc[pl.ds(pl.multiple_of(B * d + Wp, 16), B), :]
        left = sums[:, :Cr]
        left = jnp.concatenate([left[B - 1 :], left[: B - 1]], axis=0)
        right = sums[:, 2 * Cr :]
        right = jnp.concatenate([right[1:], right[:1]], axis=0)
        sums = left + sums[:, Cr : 2 * Cr] + right
        conv_s[pl.ds(pl.multiple_of(B * d, 16), B), :] = sums.astype(BF16)
        return carry

    lax.fori_loop(0, R, combine, 0)

    conv_copies = []
    for o in range(1, R):
        to = (r + o) % R
        copy = remote(
            conv_s.at[pl.ds(pl.multiple_of(B * to, 16), B), :],
            conv_r.at[r],
            conv_ss.at[o],
            conv_rs.at[o],
            at(row=to),
        )
        copy.start()
        conv_copies.append(copy)
    conv_r[r] = conv_s[pl.ds(pl.multiple_of(B * r, 16), B), :]

    for o in range(1, g):
        cross_copies[o - 1].wait()
        proj_hop(1, o).start()
        proj_hop(0, o).start()

    def attn_arrived(k):
        part = attn_quarter(k)
        return remote(part, part, attn_ss.at[k], attn_rs.at[k], at(view=(v + 1) % V))

    def attn_across(k):
        part = attn_quarter(k)
        return remote(part, part, attn_xs.at[k], attn_xr.at[k], at(row=across))

    def attn_forward(k):
        part = shard(k, mine)
        return remote(part, part, attn_fs.at[k], attn_fr.at[k], at(row=sib))

    for k in range(g):

        @pl.when(g * h + k != v)
        def _():
            attn_arrived(k).wait_recv()
            if nx > 1:
                attn_across(k).start()

    for copy in conv_copies:
        copy.wait()
    conv = jnp.concatenate([conv_r[d].astype(F32) for d in range(R)], axis=1)
    resid = (pad(x_ref[...].astype(F32).reshape(rows * W, C)) + conv + conv_bias_ref[...].reshape(1, C)).astype(
        BF16
    )
    for i in range(rows):
        out_ref[i] = resid[i * Wp : i * Wp + W]
    resid = resid.astype(F32)
    middle = jnp.mean(resid, axis=1, keepdims=True)
    gap = resid - middle
    var = jnp.mean(gap * gap, axis=1, keepdims=True)
    ny[0:B, :] = (gap * lax.rsqrt(var + EPS) * ln_gain_ref[...].reshape(1, C)).astype(BF16)
    if g * T > B:
        ny[B : g * T, :] = jnp.zeros((g * T - B, C), BF16)

    def share(k):
        return pl.ds(pl.multiple_of(k * T, 16), T)

    ally[q, h] = ny[share(q), :]
    pair_copies = []
    for o in range(1, g):
        to = (q + o) % g
        copy = remote(
            ny.at[share(to), :], ally.at[q, h], pair_ss.at[o], pair_rs.at[o], at(view=view_of(to, h))
        )
        copy.start()
        pair_copies.append(copy)

    line_hop = functools.partial(hop, lambda part, group: ally.at[part, group], line_ss, line_rs)
    line_hop(1, 0).start()
    line_hop(0, 0).start()
    proj_hop(1, 0).wait_recv()
    proj_hop(2, 0).start()
    for k in range(g):

        @pl.when(g * h + k != v)
        def _():
            if nx > 1:
                attn_across(k).wait()
            attn_forward(k).start()

    for o in range(1, g):
        line_hop(1, o - 1).wait_recv()
        line_hop(2, o - 1).start()
        pair_copies[o - 1].wait_recv()
        line_hop(1, o).start()
        line_hop(0, o).start()
    line_hop(1, g - 1).wait_recv()
    line_hop(2, g - 1).start()
    for o in range(1, g):
        proj_hop(1, o).wait_recv()
        proj_hop(2, o).start()

    for k in range(g):
        here = v // g + H * k == v

        @pl.when(here)
        def _():
            load_attn.wait()

        @pl.when(jnp.logical_not(here))
        def _():
            attn_send(k).wait_send()

        @pl.when(g * h + k != v)
        def _():
            attn_forward(k).wait()

    for copy in pair_copies:
        copy.wait_send()
    width = qkv.shape[-1]
    for o in range(g):
        line_hop(0, o).wait()
        line_hop(1, o).wait_send()
        line_hop(2, o).wait()
        part = (q + g - o) % g
        lines = ally[part].reshape(H * T, C)
        place = pl.ds(pl.multiple_of(part * (H * T), 16), H * T)
        for kind in range(3):
            qkv[kind, place, :] = dot_t(lines, attn_w[kind]).astype(BF16).astype(F32)

    for o in range(g):
        proj_hop(0, o).wait()
        proj_hop(1, o).wait_send()
        proj_hop(2, o).wait()

    def proj_across(o):
        part = proj_quarter((v + o) % V)
        return remote(part, part, proj_xs.at[o], proj_xr.at[o], at(row=across))

    def proj_forward(o):
        part = proj_block((v + o) % V, mine)
        return remote(part, part, proj_fs.at[o], proj_fr.at[o], at(row=sib))

    if nx > 1:
        for o in range(1, V):
            proj_across(o).start()

    into_heads = one_hot((width, 128), 0, head).astype(BF16)
    from_heads = one_hot((128, width), 1, head).astype(BF16)
    lane = lax.broadcasted_iota(jnp.int32, (1, 128), 1)
    scale = jnp.zeros((1, 128), F32)
    for k in range(width // head):
        scale = jnp.where(lane == k, scale_ref[h * (width // head) + k], scale)
    scale = scale * (1.0 / math.sqrt(head))

    def attend(k, carry):
        u = (v + 1 + k) % V
        query = qkv[0, pl.ds(pl.multiple_of(u * T, 16), T), :]
        product = (query[None] * qkv[1].reshape(V, T, width)).reshape(V * T, width)
        top = product.astype(BF16)
        low = (product - top.astype(F32)).astype(BF16)
        scores = jnp.dot(top, into_heads, preferred_element_type=F32) + jnp.dot(
            low, into_heads, preferred_element_type=F32
        )
        scores = (scores * scale).reshape(V, T, 128)
        weights = jnp.exp(scores - jnp.max(scores, axis=0, keepdims=True))
        weights = weights / jnp.sum(weights, axis=0, keepdims=True)
        weights = jnp.dot(
            weights.reshape(V * T, 128).astype(BF16), from_heads, preferred_element_type=F32
        )
        mixed = jnp.sum((weights * qkv[2]).reshape(V, T, width), axis=0).astype(BF16)

        @pl.when(u == v)
        def _():
            mix_r[h, share(q), :] = mixed

        @pl.when(u != v)
        def _():
            mix_s[u] = mixed
            remote(
                mix_s.at[u],
                mix_r.at[h, share(q), :],
                mix_ss.at[u],
                mix_rs.at[v],
                at(view=u),
            ).start()

        return carry

    lax.fori_loop(0, V // 2, attend, 0)
    for o in range(1, V):
        if nx > 1:
            proj_across(o).wait()
        proj_forward(o).start()
    lax.fori_loop(V // 2, V, attend, 0)

    def finish(k, carry):
        u = (v + 1 + k) % V
        remote(
            mix_s.at[u],
            mix_r.at[u % H, share(u // H), :],
            mix_ss.at[u],
            mix_rs.at[u],
            at(view=u),
        ).wait()
        return carry

    lax.fori_loop(0, V - 1, finish, 0)
    for o in range(1, V):
        proj_forward(o).wait()
    mixed = jnp.concatenate([mix_r[k].astype(F32) for k in range(H)], axis=1).astype(BF16)
    projected = jnp.dot(mixed[:B], proj_w[...], preferred_element_type=F32)
    for i in range(rows):
        out_ref[i] = (out_ref[i].astype(F32) + projected[i * Wp : i * Wp + W]).astype(BF16)


def local(
    latent,
    gn_gain,
    gn_bias,
    cam_idx,
    noise_idx,
    cam_table,
    noise_table,
    conv_w,
    conv_bias,
    ln_gain,
    attn_in,
    attn_out,
    head_scale,
):
    _, _, rows, W, C = latent.shape
    V = lax.axis_size("view")
    R = lax.axis_size("row")
    heads = head_scale.shape[0]
    head = C // heads
    H = math.gcd(V, heads)
    g = V // H
    Wp = up(W + 1, 16)
    B = rows * Wp
    T = up(-(-B // g), 16)
    Cr = conv_w.shape[-1]
    width = C // H

    film = lax.dynamic_slice_in_dim(
        cam_table, cam_idx[0, 0], 1, 0, allow_negative_indices=False
    ).astype(F32) + lax.dynamic_slice_in_dim(
        noise_table, noise_idx[0], 1, 0, allow_negative_indices=False
    ).astype(F32)

    dma = pltpu.SemaphoreType.DMA
    vmem = pl.BlockSpec(memory_space=pltpu.VMEM)
    smem = pl.BlockSpec(memory_space=pltpu.SMEM)
    hbm = pl.BlockSpec(memory_space=pl.ANY)
    out = pl.pallas_call(
        functools.partial(kernel, (V, R, H, g, T, rows, W, Wp, C, head)),
        out_shape=jax.ShapeDtypeStruct((rows, W, C), BF16),
        in_specs=[vmem] * 6 + [smem] + [hbm] * 3,
        out_specs=vmem,
        scratch_shapes=[
            pltpu.VMEM((R, 2, C), F32),
            pltpu.VMEM((R * B, C), BF16),
            pltpu.VMEM((3, 3 * Cr, C), BF16),
            pltpu.VMEM((R * B + 2 * Wp, 3 * Cr), F32),
            pltpu.VMEM((R * B, Cr), BF16),
            pltpu.VMEM((R, B, Cr), BF16),
            pltpu.VMEM((3, C // H, C), BF16),
            pltpu.VMEM((C, C), BF16),
            pltpu.VMEM((g * T, C), BF16),
            pltpu.VMEM((g, H, T, C), BF16),
            pltpu.VMEM((3, V * T, width), F32),
            pltpu.VMEM((V, T, width), BF16),
            pltpu.VMEM((H, g * T, width), BF16),
            dma((3,)),
            dma((R,)),
            dma((R,)),
            dma((R,)),
            dma((R,)),
            dma((R,)),
            dma((R,)),
            dma((R,)),
            dma((R,)),
            dma((g,)),
            dma((g,)),
            dma((g,)),
            dma((g,)),
            dma((g,)),
            dma((g,)),
            dma((3, g)),
            dma((3, g)),
            dma((V,)),
            dma((V,)),
            dma((g,)),
            dma((g,)),
            dma((3, g)),
            dma((3, g)),
            dma((V,)),
            dma((V,)),
            dma((g,)),
            dma((g,)),
            dma((V,)),
            dma((V,)),
        ],
        compiler_params=pltpu.CompilerParams(
            collective_id=0, has_side_effects=True, vmem_limit_bytes=56 * 2**20
        ),
        cost_estimate=pl.CostEstimate(
            flops=2 * R * B * C * Cr * 9, bytes_accessed=40_000_000, transcendentals=0
        ),
    )(
        latent.reshape(rows, W, C),
        film,
        gn_gain,
        gn_bias,
        conv_bias,
        ln_gain,
        head_scale,
        jnp.swapaxes(conv_w, 2, 3).reshape(3, 3 * Cr, C),
        jnp.swapaxes(attn_in, 1, 2),
        attn_out,
    )
    return out.reshape(latent.shape)


def solution(mesh):
    placed = (
        P(None, "view", "row", None, None),
        P(),
        P(),
        P(None, "view"),
        P(),
        P(),
        P(),
        P(None, None, None, "row"),
        P(),
        P(),
        P(None, None, "view"),
        P("view", None),
        P(),
    )
    return jax.shard_map(
        local,
        mesh=mesh,
        in_specs=placed,
        out_specs=P(None, "view", "row", None, None),
        check_vma=False,
    )
```

```python
import functools
import math

import jax
import jax.numpy as jnp
from jax import lax
from jax.experimental import pallas as pl
from jax.experimental.pallas import tpu as pltpu
from jax.sharding import PartitionSpec as P

GROUPS = 32
EPS = 1e-05
F32 = jnp.float32
BF16 = jnp.bfloat16


def up(n, m):
    return (n + m - 1) // m * m


def dot_t(a, b):
    return lax.dot_general(a, b, (((1,), (1,)), ((), ())), preferred_element_type=F32)


def one_hot(shape, long_axis, size):
    long = lax.broadcasted_iota(jnp.int32, shape, long_axis)
    short = lax.broadcasted_iota(jnp.int32, shape, 1 - long_axis) * size
    return (long >= short) & (long < short + size)


def kernel(
    dims,
    x_ref,
    film_ref,
    gn_gain_ref,
    gn_bias_ref,
    conv_bias_ref,
    ln_gain_ref,
    scale_ref,
    conv_hbm,
    attn_hbm,
    proj_hbm,
    out_ref,
    stat,
    act,
    conv_w,
    acc,
    conv_s,
    conv_r,
    attn_w,
    proj_w,
    ny,
    ally,
    qkv,
    mix_s,
    mix_r,
    resid_s,
    pieces,
    scores,
    soft,
    wide,
    load_sem,
    stat_ss,
    stat_rs,
    act_ss,
    act_rs,
    fwd_ss,
    fwd_rs,
    conv_ss,
    conv_rs,
    attn_ss,
    attn_rs,
    attn_fs,
    attn_fr,
    pair_ss,
    pair_rs,
    line_ss,
    line_rs,
    mix_ss,
    mix_rs,
    cross_ss,
    cross_rs,
    proj_ss,
    proj_rs,
    proj_fs,
    proj_fr,
):
    V, R, H, g, T, rows, W, Wp, C, head = dims
    B = rows * Wp
    Cr = conv_w.shape[1] // 3
    v = lax.axis_index("view")
    r = lax.axis_index("row")
    h = v % H
    q = v // H
    core = r % 2
    sib = r + 1 - 2 * core

    def at(view=None, row=None):
        return (v if view is None else view, r if row is None else row)

    def remote(src, dst, ss, rs, device):
        return pltpu.make_async_remote_copy(
            src_ref=src,
            dst_ref=dst,
            send_sem=ss,
            recv_sem=rs,
            device_id=device,
            device_id_type=pl.DeviceIdType.MESH,
        )

    load_conv = pltpu.make_async_copy(conv_hbm, conv_w, load_sem.at[0])
    Ca = proj_hbm.shape[0]
    half = C // 2
    mine = pl.ds(pl.multiple_of(core * half, half), half)

    def proj_block(view, columns):
        return proj_w.at[pl.ds(pl.multiple_of(view * Ca, 16), Ca), columns]

    load_proj = pltpu.make_async_copy(proj_hbm, proj_block(v, slice(None)), load_sem.at[2])
    load_proj.start()
    load_conv.start()
    barrier = pltpu.get_barrier_semaphore()
    for o in range(1, R):
        pl.semaphore_signal(
            barrier, inc=1, device_id=at(row=(r + o) % R), device_id_type=pl.DeviceIdType.MESH
        )
    for o in range(1, V):
        pl.semaphore_signal(
            barrier, inc=1, device_id=at(view=(v + o) % V), device_id_type=pl.DeviceIdType.MESH
        )

    lanes = [slice(k, min(k + 256, C)) for k in range(0, C, 256)]
    size = C // GROUPS
    into = one_hot((C, 128), 0, size).astype(F32).astype(BF16)
    back = one_hot((128, C), 1, size).astype(F32).astype(BF16)
    count = rows * W * size

    def sum_dot(values, ones):
        line = lax.broadcasted_iota(jnp.int32, (8, values.shape[1]), 0)
        values = jnp.broadcast_to(values, line.shape)
        top = values.astype(BF16).astype(F32)
        rest = values - top
        middle = rest.astype(BF16).astype(F32)
        low = rest - middle
        pieces = jnp.where(line == 0, top, jnp.where(line == 1, middle, low))
        pieces = jnp.where(line < 3, pieces, 0.0).astype(BF16)
        return jnp.sum(
            jnp.dot(pieces, ones, preferred_element_type=F32), axis=0, keepdims=True
        )

    def spread(total):
        return sum_dot(sum_dot(total, into), back)

    def by_lanes(total):
        parts = []
        for part in lanes:
            parts.append(sum(total(x_ref[i, :, part].astype(F32), part) for i in range(rows)))
        return jnp.concatenate(parts, axis=1)

    def squares(x, part):
        off = x - mean_here[:, part]
        return jnp.sum(off * off, axis=0, keepdims=True)

    mean_here = spread(by_lanes(lambda x, part: jnp.sum(x, axis=0, keepdims=True)))
    mean_here = mean_here * (1.0 / count)
    square_here = spread(by_lanes(squares))
    stat[r, 0:1, :] = mean_here
    stat[r, 1:2, :] = square_here

    pl.semaphore_wait(barrier, R - 1 + V - 1)

    stat_copies = []
    for o in range(1, R):
        copy = remote(
            stat.at[r], stat.at[r], stat_ss.at[o], stat_rs.at[o], at(row=(r + o) % R)
        )
        copy.start()
        stat_copies.append(copy)

    beside = h + 1 - 2 * (h % 2)
    above = (h + 2) % H

    def view_of(part, group):
        return part * H + group

    def hop(slot, ss, rs, way, o):
        part = slot((q + g - o) % g, above if way == 2 else h)
        return remote(
            part,
            part,
            ss.at[way, o],
            rs.at[way, o],
            at(view=view_of(q, above if way == 1 else beside)),
        )

    def proj_slot(part, group):
        return proj_block(view_of(part, group), mine)

    proj_hop = functools.partial(hop, proj_slot, proj_ss, proj_rs)
    load_proj.wait()
    proj_hop(1, 0).start()
    proj_hop(0, 0).start()
    cross_copies = []
    for o in range(1, g):
        copy = remote(
            proj_slot(q, h),
            proj_slot(q, h),
            cross_ss.at[o],
            cross_rs.at[o],
            at(view=view_of((q + o) % g, h)),
        )
        copy.start()
        cross_copies.append(copy)

    def shard(k, columns):
        return attn_w.at[:, pl.ds(pl.multiple_of(k * Ca, 16), Ca), columns]

    def attn_send(k):
        return remote(
            attn_hbm.at[:, :, mine],
            shard(v % g, mine),
            attn_ss.at[k],
            attn_rs.at[v % g],
            at(view=v // g + H * k),
        )

    load_attn = pltpu.make_async_copy(attn_hbm, shard(v % g, slice(None)), load_sem.at[1])
    for k in range(g):
        here = v // g + H * k == v

        @pl.when(here)
        def _():
            load_attn.start()

        @pl.when(jnp.logical_not(here))
        def _():
            attn_send(k).start()

    for copy in stat_copies:
        copy.wait()
    means = [stat[d, 0:1, :] for d in range(R)]
    mean = sum(means[1:], means[0]) * (1.0 / R)
    total = jnp.zeros((1, C), F32)
    for d in range(R):
        gap = means[d] - mean
        total = total + stat[d, 1:2, :] + count * (gap * gap)
    rstd = lax.rsqrt(total * (1.0 / (count * R)) + EPS)
    film_gain = 1.0 + film_ref[:, :C]
    gain = rstd * (gn_gain_ref[...].reshape(1, C) * film_gain)
    shift = gn_bias_ref[...].reshape(1, C) * film_gain + film_ref[:, C:]
    none = jnp.zeros((Wp - W, 256), F32)
    for i in range(rows):
        for part in lanes:
            x = x_ref[i, :, part].astype(F32)
            hidden = (x - mean[:, part]) * gain[:, part] + shift[:, part]
            hidden = hidden / (1.0 + jnp.exp(-hidden))
            hidden = jnp.concatenate([hidden, none[:, : hidden.shape[1]]], axis=0)
            line = pl.ds(pl.multiple_of(B * r + i * Wp, 16), Wp)
            act[line, part] = hidden.astype(BF16)

    def block(d):
        return act.at[pl.ds(pl.multiple_of(B * d, 16), B), :]

    act_copies = []
    for o in range(1, R // 2):
        copy = remote(
            block(r), block(r), act_ss.at[o], act_rs.at[o], at(row=(r + 2 * o) % R)
        )
        copy.start()
        act_copies.append(copy)
    forwards = [remote(block(r), block(r), fwd_ss.at[0], fwd_rs.at[0], at(row=sib))]
    forwards[0].start()

    acc[...] = jnp.zeros(acc.shape, F32)

    def convolve(pair):
        start = pl.multiple_of(pair * 2 * B, 16)

        def taps(i, carry):
            lines = act[pl.ds(start, 2 * B), :]
            out = pl.ds(pl.multiple_of(start + (2 - i) * Wp, 16), 2 * B)
            acc[out, :] += dot_t(lines, conv_w[i])
            return carry

        lax.fori_loop(0, 3, taps, 0)

    load_conv.wait()
    forwards[0].wait_recv()
    convolve(r // 2)
    for o in range(1, R // 2):
        act_copies[o - 1].wait_recv()
        source = (r + R - 2 * o) % R
        copy = remote(
            block(source), block(source), fwd_ss.at[o], fwd_rs.at[o], at(row=sib)
        )
        copy.start()
        forwards.append(copy)
    for o in range(1, R // 2):
        forwards[o].wait_recv()
        convolve((r // 2 + R // 2 - o) % (R // 2))

    for copy in act_copies + forwards:
        copy.wait_send()

    def combine(d):
        sums = acc[pl.ds(pl.multiple_of(B * d + Wp, 16), B), :]
        left = sums[:, :Cr]
        left = jnp.concatenate([left[B - 1 :], left[: B - 1]], axis=0)
        right = sums[:, 2 * Cr :]
        right = jnp.concatenate([right[1:], right[:1]], axis=0)
        return (left + sums[:, Cr : 2 * Cr] + right).astype(BF16)

    def conv_send(o):
        return remote(
            conv_s.at[o], conv_r.at[r], conv_ss.at[o], conv_rs.at[o], at(row=(r + o) % R)
        )

    def return_block(o, carry):
        conv_s[o] = combine((r + o) % R)
        conv_send(o).start()
        return carry

    lax.fori_loop(1, R, return_block, 0)
    conv_r[r] = combine(r)
    for i in range(rows):
        resid_s[i * Wp : i * Wp + W, :] = x_ref[i]
        resid_s[i * Wp + W : (i + 1) * Wp, :] = jnp.zeros((Wp - W, C), BF16)
    conv_copies = [conv_send(o) for o in range(1, R)]

    for o in range(1, g):
        cross_copies[o - 1].wait()
        proj_hop(1, o).start()
        proj_hop(0, o).start()

    def attn_arrived(k):
        part = shard(k, mine)
        return remote(part, part, attn_ss.at[k], attn_rs.at[k], at(view=(v + 1) % V))

    def attn_forward(k):
        part = shard(k, mine)
        return remote(part, part, attn_fs.at[k], attn_fr.at[k], at(row=sib))

    for k in range(g):

        @pl.when(g * h + k != v)
        def _():
            attn_arrived(k).wait_recv()
            attn_forward(k).start()

    for copy in conv_copies:
        copy.wait()
    bias = conv_bias_ref[...].reshape(1, C)
    scale_y = ln_gain_ref[...].reshape(1, C)
    for start in range(0, B, 16):
        lines = slice(start, start + 16)
        conv = jnp.concatenate([conv_r[d, lines, :].astype(F32) for d in range(R)], axis=1)
        resid = (resid_s[lines, :].astype(F32) + conv + bias).astype(BF16)
        resid_s[lines, :] = resid
        resid = resid.astype(F32)
        middle = jnp.mean(resid, axis=1, keepdims=True)
        gap = resid - middle
        var = jnp.mean(gap * gap, axis=1, keepdims=True)
        ny[lines, :] = (gap * lax.rsqrt(var + EPS) * scale_y).astype(BF16)
    if g * T > B:
        ny[B : g * T, :] = jnp.zeros((g * T - B, C), BF16)

    def share(k):
        return pl.ds(pl.multiple_of(k * T, 16), T)

    ally[q, h] = ny[share(q), :]
    pair_copies = []
    for o in range(1, g):
        to = (q + o) % g
        copy = remote(
            ny.at[share(to), :], ally.at[q, h], pair_ss.at[o], pair_rs.at[o], at(view=view_of(to, h))
        )
        copy.start()
        pair_copies.append(copy)

    line_hop = functools.partial(hop, lambda part, group: ally.at[part, group], line_ss, line_rs)
    line_hop(1, 0).start()
    line_hop(0, 0).start()
    proj_hop(1, 0).wait_recv()
    proj_hop(2, 0).start()
    for o in range(1, g):
        line_hop(1, o - 1).wait_recv()
        line_hop(2, o - 1).start()
        pair_copies[o - 1].wait_recv()
        line_hop(1, o).start()
        line_hop(0, o).start()
    line_hop(1, g - 1).wait_recv()
    line_hop(2, g - 1).start()
    for o in range(1, g):
        proj_hop(1, o).wait_recv()
        proj_hop(2, o).start()

    for k in range(g):
        here = v // g + H * k == v

        @pl.when(here)
        def _():
            load_attn.wait()

        @pl.when(jnp.logical_not(here))
        def _():
            attn_send(k).wait_send()

        @pl.when(g * h + k != v)
        def _():
            attn_forward(k).wait()

    for copy in pair_copies:
        copy.wait_send()
    width = qkv.shape[-1]
    for o in range(g):
        line_hop(0, o).wait()
        line_hop(1, o).wait_send()
        line_hop(2, o).wait()
        part = (q + g - o) % g
        lines = ally[part].reshape(H * T, C)
        place = pl.ds(pl.multiple_of(part * (H * T), 16), H * T)
        for kind in range(3):
            qkv[kind, place, :] = dot_t(lines, attn_w[kind]).astype(BF16).astype(F32)

    for o in range(g):
        proj_hop(0, o).wait()
        proj_hop(1, o).wait_send()
        proj_hop(2, o).wait()

    def proj_forward(o):
        part = proj_block((v + o) % V, mine)
        return remote(part, part, proj_fs.at[o], proj_fr.at[o], at(row=sib))

    for o in range(1, V):
        proj_forward(o).start()

    into_heads = one_hot((width, 128), 0, head).astype(BF16)
    from_heads = one_hot((128, width), 1, head).astype(BF16)
    lane = lax.broadcasted_iota(jnp.int32, (1, 128), 1)
    scale = jnp.zeros((1, 128), F32)
    for k in range(width // head):
        scale = jnp.where(lane == k, scale_ref[h * (width // head) + k], scale)
    scale = scale * (1.0 / math.sqrt(head))

    def attend(k, carry):
        u = (v + 1 + k) % V
        base = pl.multiple_of(u * T, 16)
        for start in range(0, T, 16):
            query = qkv[0, pl.ds(base + start, 16), :]
            for w in range(V):
                lines = slice(w * T + start, w * T + start + 16)
                product = query * qkv[1, lines, :]
                top = product.astype(BF16)
                pieces[0, lines, :] = top
                pieces[1, lines, :] = (product - top.astype(F32)).astype(BF16)
        scores[...] = jnp.dot(
            pieces[...].reshape(2 * V * T, width), into_heads, preferred_element_type=F32
        )
        for start in range(0, T, 16):
            several = []
            for w in range(V):
                line = w * T + start
                several.append(
                    (scores[line : line + 16] + scores[V * T + line : V * T + line + 16]) * scale
                )
            peak = functools.reduce(jnp.maximum, several)
            several = [jnp.exp(one - peak) for one in several]
            inverse = 1.0 / sum(several)
            for w in range(V):
                line = w * T + start
                soft[line : line + 16] = (several[w] * inverse).astype(BF16)
        wide[...] = jnp.dot(soft[...], from_heads, preferred_element_type=F32)
        mixed = []
        for start in range(0, T, 16):
            total = 0.0
            for w in range(V):
                lines = slice(w * T + start, w * T + start + 16)
                total = total + wide[lines, :] * qkv[2, lines, :]
            mixed.append(total.astype(BF16))
        mixed = jnp.concatenate(mixed, axis=0)

        @pl.when(u == v)
        def _():
            mix_r[h, share(q), :] = mixed

        @pl.when(u != v)
        def _():
            mix_s[u] = mixed
            remote(
                mix_s.at[u],
                mix_r.at[h, share(q), :],
                mix_ss.at[u],
                mix_rs.at[v],
                at(view=u),
            ).start()

        return carry

    lax.fori_loop(0, V, attend, 0)

    def finish(k, carry):
        u = (v + 1 + k) % V
        remote(
            mix_s.at[u],
            mix_r.at[u % H, share(u // H), :],
            mix_ss.at[u],
            mix_rs.at[u],
            at(view=u),
        ).wait()
        return carry

    lax.fori_loop(0, V - 1, finish, 0)
    for o in range(1, V):
        proj_forward(o).wait()
    mixed = jnp.concatenate([mix_r[k].astype(F32) for k in range(H)], axis=1).astype(BF16)
    projected = jnp.dot(mixed[:B], proj_w[...], preferred_element_type=F32)
    for i in range(rows):
        out_ref[i] = (
            resid_s[i * Wp : i * Wp + W].astype(F32) + projected[i * Wp : i * Wp + W]
        ).astype(BF16)


def local(
    latent,
    gn_gain,
    gn_bias,
    cam_idx,
    noise_idx,
    cam_table,
    noise_table,
    conv_w,
    conv_bias,
    ln_gain,
    attn_in,
    attn_out,
    head_scale,
):
    _, _, rows, W, C = latent.shape
    V = lax.axis_size("view")
    R = lax.axis_size("row")
    heads = head_scale.shape[0]
    head = C // heads
    H = math.gcd(V, heads)
    g = V // H
    Wp = up(W + 1, 16)
    B = rows * Wp
    T = up(-(-B // g), 16)
    Cr = conv_w.shape[-1]
    width = C // H

    film = lax.dynamic_slice_in_dim(
        cam_table, cam_idx[0, 0], 1, 0, allow_negative_indices=False
    ).astype(F32) + lax.dynamic_slice_in_dim(
        noise_table, noise_idx[0], 1, 0, allow_negative_indices=False
    ).astype(F32)

    dma = pltpu.SemaphoreType.DMA
    vmem = pl.BlockSpec(memory_space=pltpu.VMEM)
    smem = pl.BlockSpec(memory_space=pltpu.SMEM)
    hbm = pl.BlockSpec(memory_space=pl.ANY)
    out = pl.pallas_call(
        functools.partial(kernel, (V, R, H, g, T, rows, W, Wp, C, head)),
        out_shape=jax.ShapeDtypeStruct((rows, W, C), BF16),
        in_specs=[vmem] * 6 + [smem] + [hbm] * 3,
        out_specs=vmem,
        scratch_shapes=[
            pltpu.VMEM((R, 2, C), F32),
            pltpu.VMEM((R * B, C), BF16),
            pltpu.VMEM((3, 3 * Cr, C), BF16),
            pltpu.VMEM((R * B + 2 * Wp, 3 * Cr), F32),
            pltpu.VMEM((R, B, Cr), BF16),
            pltpu.VMEM((R, B, Cr), BF16),
            pltpu.VMEM((3, C // H, C), BF16),
            pltpu.VMEM((C, C), BF16),
            pltpu.VMEM((g * T, C), BF16),
            pltpu.VMEM((g, H, T, C), BF16),
            pltpu.VMEM((3, V * T, width), F32),
            pltpu.VMEM((V, T, width), BF16),
            pltpu.VMEM((H, g * T, width), BF16),
            pltpu.VMEM((B, C), BF16),
            pltpu.VMEM((2, V * T, width), BF16),
            pltpu.VMEM((2 * V * T, 128), F32),
            pltpu.VMEM((V * T, 128), BF16),
            pltpu.VMEM((V * T, width), F32),
            dma((3,)),
            dma((R,)),
            dma((R,)),
            dma((R,)),
            dma((R,)),
            dma((R,)),
            dma((R,)),
            dma((R,)),
            dma((R,)),
            dma((g,)),
            dma((g,)),
            dma((g,)),
            dma((g,)),
            dma((g,)),
            dma((g,)),
            dma((3, g)),
            dma((3, g)),
            dma((V,)),
            dma((V,)),
            dma((g,)),
            dma((g,)),
            dma((3, g)),
            dma((3, g)),
            dma((V,)),
            dma((V,)),
        ],
        compiler_params=pltpu.CompilerParams(
            collective_id=0, has_side_effects=True, vmem_limit_bytes=56 * 2**20
        ),
        cost_estimate=pl.CostEstimate(
            flops=2 * R * B * C * Cr * 9, bytes_accessed=40_000_000, transcendentals=0
        ),
    )(
        latent.reshape(rows, W, C),
        film,
        gn_gain,
        gn_bias,
        conv_bias,
        ln_gain,
        head_scale,
        jnp.swapaxes(conv_w, 2, 3).reshape(3, 3 * Cr, C),
        jnp.swapaxes(attn_in, 1, 2),
        attn_out,
    )
    return out.reshape(latent.shape)


def solution(mesh):
    placed = (
        P(None, "view", "row", None, None),
        P(),
        P(),
        P(None, "view"),
        P(),
        P(),
        P(),
        P(None, None, None, "row"),
        P(),
        P(),
        P(None, None, "view"),
        P("view", None),
        P(),
    )
    return jax.shard_map(
        local,
        mesh=mesh,
        in_specs=placed,
        out_specs=P(None, "view", "row", None, None),
        check_vma=False,
    )
```

```python
import functools
import math

import jax
import jax.numpy as jnp
from jax import lax
from jax.experimental import pallas as pl
from jax.experimental.pallas import tpu as pltpu
from jax.sharding import PartitionSpec as P

GROUPS = 32
EPS = 1e-05
F32 = jnp.float32
BF16 = jnp.bfloat16


def up(n, m):
    return (n + m - 1) // m * m


def dot_t(a, b):
    return lax.dot_general(a, b, (((1,), (1,)), ((), ())), preferred_element_type=F32)


def one_hot(shape, long_axis, size):
    long = lax.broadcasted_iota(jnp.int32, shape, long_axis)
    short = lax.broadcasted_iota(jnp.int32, shape, 1 - long_axis) * size
    return (long >= short) & (long < short + size)


def kernel(
    dims,
    x_ref,
    film_ref,
    gn_gain_ref,
    gn_bias_ref,
    conv_bias_ref,
    ln_gain_ref,
    scale_ref,
    conv_hbm,
    attn_hbm,
    proj_hbm,
    out_ref,
    stat,
    act,
    conv_w,
    acc,
    conv_s,
    conv_r,
    attn_w,
    proj_w,
    ny,
    ally,
    qkv,
    mix_s,
    mix_r,
    resid_s,
    pieces,
    scores,
    soft,
    wide,
    load_sem,
    stat_ss,
    stat_rs,
    act_ss,
    act_rs,
    fwd_ss,
    fwd_rs,
    conv_ss,
    conv_rs,
    attn_ss,
    attn_rs,
    attn_fs,
    attn_fr,
    pair_ss,
    pair_rs,
    line_ss,
    line_rs,
    mix_ss,
    mix_rs,
    cross_ss,
    cross_rs,
    proj_ss,
    proj_rs,
    proj_fs,
    proj_fr,
    attn_xs,
    attn_xr,
    proj_xs,
    proj_xr,
):
    V, R, H, g, T, rows, W, Wp, C, head = dims
    B = rows * Wp
    Cr = conv_w.shape[1] // 3
    v = lax.axis_index("view")
    r = lax.axis_index("row")
    h = v % H
    q = v // H
    core = r % 2
    sib = r + 1 - 2 * core

    def at(view=None, row=None):
        return (v if view is None else view, r if row is None else row)

    def remote(src, dst, ss, rs, device):
        return pltpu.make_async_remote_copy(
            src_ref=src,
            dst_ref=dst,
            send_sem=ss,
            recv_sem=rs,
            device_id=device,
            device_id_type=pl.DeviceIdType.MESH,
        )

    load_conv = pltpu.make_async_copy(conv_hbm, conv_w, load_sem.at[0])
    Ca = proj_hbm.shape[0]
    half = C // 2
    mine = pl.ds(pl.multiple_of(core * half, half), half)

    nx = 2 if R == 4 and Ca % 32 == 0 else 1
    Cq = Ca // nx
    first = (r // 2) % nx * Cq
    across = (r + 2) % R

    def proj_block(view, columns):
        return proj_w.at[pl.ds(pl.multiple_of(view * Ca, 16), Ca), columns]

    def proj_quarter(view):
        return proj_w.at[pl.ds(pl.multiple_of(view * Ca + first, 16), Cq), mine]

    load_proj = pltpu.make_async_copy(proj_hbm, proj_block(v, slice(None)), load_sem.at[2])
    load_proj.start()
    load_conv.start()
    barrier = pltpu.get_barrier_semaphore()
    for o in range(1, R):
        pl.semaphore_signal(
            barrier, inc=1, device_id=at(row=(r + o) % R), device_id_type=pl.DeviceIdType.MESH
        )
    for o in range(1, V):
        pl.semaphore_signal(
            barrier, inc=1, device_id=at(view=(v + o) % V), device_id_type=pl.DeviceIdType.MESH
        )

    lanes = [slice(k, min(k + 256, C)) for k in range(0, C, 256)]
    size = C // GROUPS
    into = one_hot((C, 128), 0, size).astype(F32).astype(BF16)
    back = one_hot((128, C), 1, size).astype(F32).astype(BF16)
    count = rows * W * size

    def sum_dot(values, ones):
        line = lax.broadcasted_iota(jnp.int32, (8, values.shape[1]), 0)
        values = jnp.broadcast_to(values, line.shape)
        top = values.astype(BF16).astype(F32)
        rest = values - top
        middle = rest.astype(BF16).astype(F32)
        low = rest - middle
        pieces = jnp.where(line == 0, top, jnp.where(line == 1, middle, low))
        pieces = jnp.where(line < 3, pieces, 0.0).astype(BF16)
        return jnp.sum(
            jnp.dot(pieces, ones, preferred_element_type=F32), axis=0, keepdims=True
        )

    def spread(total):
        return sum_dot(sum_dot(total, into), back)

    def by_lanes(total):
        parts = []
        for part in lanes:
            parts.append(sum(total(x_ref[i, :, part].astype(F32), part) for i in range(rows)))
        return jnp.concatenate(parts, axis=1)

    def squares(x, part):
        off = x - mean_here[:, part]
        return jnp.sum(off * off, axis=0, keepdims=True)

    mean_here = spread(by_lanes(lambda x, part: jnp.sum(x, axis=0, keepdims=True)))
    mean_here = mean_here * (1.0 / count)
    square_here = spread(by_lanes(squares))
    stat[r, 0:1, :] = mean_here
    stat[r, 1:2, :] = square_here

    pl.semaphore_wait(barrier, R - 1 + V - 1)

    stat_copies = []
    for o in range(1, R):
        copy = remote(
            stat.at[r], stat.at[r], stat_ss.at[o], stat_rs.at[o], at(row=(r + o) % R)
        )
        copy.start()
        stat_copies.append(copy)

    beside = h + 1 - 2 * (h % 2)
    above = (h + 2) % H

    def view_of(part, group):
        return part * H + group

    def hop(slot, ss, rs, way, o):
        part = slot((q + g - o) % g, above if way == 2 else h)
        return remote(
            part,
            part,
            ss.at[way, o],
            rs.at[way, o],
            at(view=view_of(q, above if way == 1 else beside)),
        )

    def proj_slot(part, group):
        return proj_quarter(view_of(part, group))

    proj_hop = functools.partial(hop, proj_slot, proj_ss, proj_rs)
    load_proj.wait()
    proj_hop(1, 0).start()
    proj_hop(0, 0).start()
    cross_copies = []
    for o in range(1, g):
        copy = remote(
            proj_slot(q, h),
            proj_slot(q, h),
            cross_ss.at[o],
            cross_rs.at[o],
            at(view=view_of((q + o) % g, h)),
        )
        copy.start()
        cross_copies.append(copy)

    def shard(k, columns):
        return attn_w.at[:, pl.ds(pl.multiple_of(k * Ca, 16), Ca), columns]

    def attn_quarter(k):
        return attn_w.at[:, pl.ds(pl.multiple_of(k * Ca + first, 16), Cq), mine]

    def attn_send(k):
        return remote(
            attn_hbm.at[:, pl.ds(pl.multiple_of(first, 16), Cq), mine],
            attn_quarter(v % g),
            attn_ss.at[k],
            attn_rs.at[v % g],
            at(view=v // g + H * k),
        )

    load_attn = pltpu.make_async_copy(attn_hbm, shard(v % g, slice(None)), load_sem.at[1])
    for k in range(g):
        here = v // g + H * k == v

        @pl.when(here)
        def _():
            load_attn.start()

        @pl.when(jnp.logical_not(here))
        def _():
            attn_send(k).start()

    for copy in stat_copies:
        copy.wait()
    means = [stat[d, 0:1, :] for d in range(R)]
    mean = sum(means[1:], means[0]) * (1.0 / R)
    total = jnp.zeros((1, C), F32)
    for d in range(R):
        gap = means[d] - mean
        total = total + stat[d, 1:2, :] + count * (gap * gap)
    rstd = lax.rsqrt(total * (1.0 / (count * R)) + EPS)
    film_gain = 1.0 + film_ref[:, :C]
    gain = rstd * (gn_gain_ref[...].reshape(1, C) * film_gain)
    shift = gn_bias_ref[...].reshape(1, C) * film_gain + film_ref[:, C:]
    none = jnp.zeros((Wp - W, 256), F32)
    for i in range(rows):
        for part in lanes:
            x = x_ref[i, :, part].astype(F32)
            hidden = (x - mean[:, part]) * gain[:, part] + shift[:, part]
            hidden = hidden / (1.0 + jnp.exp(-hidden))
            hidden = jnp.concatenate([hidden, none[:, : hidden.shape[1]]], axis=0)
            line = pl.ds(pl.multiple_of(B * r + i * Wp, 16), Wp)
            act[line, part] = hidden.astype(BF16)

    def block(d):
        return act.at[pl.ds(pl.multiple_of(B * d, 16), B), :]

    act_copies = []
    for o in range(1, R // 2):
        copy = remote(
            block(r), block(r), act_ss.at[o], act_rs.at[o], at(row=(r + 2 * o) % R)
        )
        copy.start()
        act_copies.append(copy)
    forwards = [remote(block(r), block(r), fwd_ss.at[0], fwd_rs.at[0], at(row=sib))]
    forwards[0].start()

    for o in range(1, g):
        cross_copies[o - 1].wait()
        proj_hop(1, o).start()
        proj_hop(0, o).start()
    proj_hop(1, 0).wait_recv()
    proj_hop(2, 0).start()

    acc[...] = jnp.zeros(acc.shape, F32)

    def convolve(pair):
        start = pl.multiple_of(pair * 2 * B, 16)

        def taps(i, carry):
            lines = act[pl.ds(start, 2 * B), :]
            out = pl.ds(pl.multiple_of(start + (2 - i) * Wp, 16), 2 * B)
            acc[out, :] += dot_t(lines, conv_w[i])
            return carry

        lax.fori_loop(0, 3, taps, 0)

    load_conv.wait()
    forwards[0].wait_recv()
    convolve(r // 2)
    for o in range(1, g):
        proj_hop(1, o).wait_recv()
        proj_hop(2, o).start()
    for o in range(1, R // 2):
        act_copies[o - 1].wait_recv()
        source = (r + R - 2 * o) % R
        copy = remote(
            block(source), block(source), fwd_ss.at[o], fwd_rs.at[o], at(row=sib)
        )
        copy.start()
        forwards.append(copy)
    for o in range(1, R // 2):
        forwards[o].wait_recv()
        convolve((r // 2 + R // 2 - o) % (R // 2))

    for copy in act_copies + forwards:
        copy.wait_send()

    def combine(d):
        sums = acc[pl.ds(pl.multiple_of(B * d + Wp, 16), B), :]
        left = sums[:, :Cr]
        left = jnp.concatenate([left[B - 1 :], left[: B - 1]], axis=0)
        right = sums[:, 2 * Cr :]
        right = jnp.concatenate([right[1:], right[:1]], axis=0)
        return (left + sums[:, Cr : 2 * Cr] + right).astype(BF16)

    def conv_send(o):
        return remote(
            conv_s.at[o], conv_r.at[r], conv_ss.at[o], conv_rs.at[o], at(row=(r + o) % R)
        )

    def return_block(o, carry):
        conv_s[o] = combine((r + o) % R)
        conv_send(o).start()
        return carry

    lax.fori_loop(1, R, return_block, 0)
    conv_r[r] = combine(r)
    for i in range(rows):
        resid_s[i * Wp : i * Wp + W, :] = x_ref[i]
        resid_s[i * Wp + W : (i + 1) * Wp, :] = jnp.zeros((Wp - W, C), BF16)
    conv_copies = [conv_send(o) for o in range(1, R)]

    def attn_arrived(k):
        part = attn_quarter(k)
        return remote(part, part, attn_ss.at[k], attn_rs.at[k], at(view=(v + 1) % V))

    def attn_across(k):
        part = attn_quarter(k)
        return remote(part, part, attn_xs.at[k], attn_xr.at[k], at(row=across))

    def attn_forward(k):
        part = shard(k, mine)
        return remote(part, part, attn_fs.at[k], attn_fr.at[k], at(row=sib))

    for k in range(g):

        @pl.when(g * h + k != v)
        def _():
            attn_arrived(k).wait_recv()
            if nx > 1:
                attn_across(k).start()

    for copy in conv_copies:
        copy.wait()
    bias = conv_bias_ref[...].reshape(1, C)
    scale_y = ln_gain_ref[...].reshape(1, C)
    for start in range(0, B, 16):
        lines = slice(start, start + 16)
        conv = jnp.concatenate([conv_r[d, lines, :].astype(F32) for d in range(R)], axis=1)
        resid = (resid_s[lines, :].astype(F32) + conv + bias).astype(BF16)
        resid_s[lines, :] = resid
        resid = resid.astype(F32)
        middle = jnp.mean(resid, axis=1, keepdims=True)
        gap = resid - middle
        var = jnp.mean(gap * gap, axis=1, keepdims=True)
        ny[lines, :] = (gap * lax.rsqrt(var + EPS) * scale_y).astype(BF16)
    if g * T > B:
        ny[B : g * T, :] = jnp.zeros((g * T - B, C), BF16)

    def share(k):
        return pl.ds(pl.multiple_of(k * T, 16), T)

    ally[q, h] = ny[share(q), :]
    pair_copies = []
    for o in range(1, g):
        to = (q + o) % g
        copy = remote(
            ny.at[share(to), :], ally.at[q, h], pair_ss.at[o], pair_rs.at[o], at(view=view_of(to, h))
        )
        copy.start()
        pair_copies.append(copy)

    line_hop = functools.partial(hop, lambda part, group: ally.at[part, group], line_ss, line_rs)
    line_hop(1, 0).start()
    line_hop(0, 0).start()
    for o in range(1, g):
        line_hop(1, o - 1).wait_recv()
        line_hop(2, o - 1).start()
        pair_copies[o - 1].wait_recv()
        line_hop(1, o).start()
        line_hop(0, o).start()
    line_hop(1, g - 1).wait_recv()
    line_hop(2, g - 1).start()
    for o in range(g):
        proj_hop(0, o).wait()
        proj_hop(1, o).wait_send()
        proj_hop(2, o).wait()

    def proj_across(o):
        part = proj_quarter((v + o) % V)
        return remote(part, part, proj_xs.at[o], proj_xr.at[o], at(row=across))

    def proj_forward(o):
        part = proj_block((v + o) % V, mine)
        return remote(part, part, proj_fs.at[o], proj_fr.at[o], at(row=sib))

    for k in range(g):

        @pl.when(g * h + k != v)
        def _():
            if nx > 1:
                attn_across(k).wait()
            attn_forward(k).start()

    if nx > 1:
        for o in range(1, V):
            proj_across(o).start()

    for k in range(g):
        here = v // g + H * k == v

        @pl.when(here)
        def _():
            load_attn.wait()

        @pl.when(jnp.logical_not(here))
        def _():
            attn_send(k).wait_send()

        @pl.when(g * h + k != v)
        def _():
            attn_forward(k).wait()

    for copy in pair_copies:
        copy.wait_send()
    width = qkv.shape[-1]
    for o in range(g):
        line_hop(0, o).wait()
        line_hop(1, o).wait_send()
        line_hop(2, o).wait()
        part = (q + g - o) % g
        lines = ally[part].reshape(H * T, C)
        place = pl.ds(pl.multiple_of(part * (H * T), 16), H * T)
        for kind in range(3):
            qkv[kind, place, :] = dot_t(lines, attn_w[kind]).astype(BF16).astype(F32)

    into_heads = one_hot((width, 128), 0, head).astype(BF16)
    from_heads = one_hot((128, width), 1, head).astype(BF16)
    lane = lax.broadcasted_iota(jnp.int32, (1, 128), 1)
    scale = jnp.zeros((1, 128), F32)
    for k in range(width // head):
        scale = jnp.where(lane == k, scale_ref[h * (width // head) + k], scale)
    scale = scale * (1.0 / math.sqrt(head))

    def attend(k, carry):
        u = (v + 1 + k) % V
        base = pl.multiple_of(u * T, 16)
        for start in range(0, T, 16):
            query = qkv[0, pl.ds(base + start, 16), :]
            for w in range(V):
                lines = slice(w * T + start, w * T + start + 16)
                product = query * qkv[1, lines, :]
                top = product.astype(BF16)
                pieces[0, lines, :] = top
                pieces[1, lines, :] = (product - top.astype(F32)).astype(BF16)
        scores[...] = jnp.dot(
            pieces[...].reshape(2 * V * T, width), into_heads, preferred_element_type=F32
        )
        for start in range(0, T, 16):
            several = []
            for w in range(V):
                line = w * T + start
                several.append(
                    (scores[line : line + 16] + scores[V * T + line : V * T + line + 16]) * scale
                )
            peak = functools.reduce(jnp.maximum, several)
            several = [jnp.exp(one - peak) for one in several]
            inverse = 1.0 / sum(several)
            for w in range(V):
                line = w * T + start
                soft[line : line + 16] = (several[w] * inverse).astype(BF16)
        wide[...] = jnp.dot(soft[...], from_heads, preferred_element_type=F32)
        mixed = []
        for start in range(0, T, 16):
            total = 0.0
            for w in range(V):
                lines = slice(w * T + start, w * T + start + 16)
                total = total + wide[lines, :] * qkv[2, lines, :]
            mixed.append(total.astype(BF16))
        mixed = jnp.concatenate(mixed, axis=0)

        @pl.when(u == v)
        def _():
            mix_r[h, share(q), :] = mixed

        @pl.when(u != v)
        def _():
            mix_s[u] = mixed
            remote(
                mix_s.at[u],
                mix_r.at[h, share(q), :],
                mix_ss.at[u],
                mix_rs.at[v],
                at(view=u),
            ).start()

        return carry

    lax.fori_loop(0, V // 2, attend, 0)
    for o in range(1, V):
        if nx > 1:
            proj_across(o).wait()
        proj_forward(o).start()
    lax.fori_loop(V // 2, V, attend, 0)

    def finish(k, carry):
        u = (v + 1 + k) % V
        remote(
            mix_s.at[u],
            mix_r.at[u % H, share(u // H), :],
            mix_ss.at[u],
            mix_rs.at[u],
            at(view=u),
        ).wait()
        return carry

    lax.fori_loop(0, V - 1, finish, 0)
    for o in range(1, V):
        proj_forward(o).wait()
    mixed = jnp.concatenate([mix_r[k].astype(F32) for k in range(H)], axis=1).astype(BF16)
    projected = jnp.dot(mixed[:B], proj_w[...], preferred_element_type=F32)
    for i in range(rows):
        out_ref[i] = (
            resid_s[i * Wp : i * Wp + W].astype(F32) + projected[i * Wp : i * Wp + W]
        ).astype(BF16)


def local(
    latent,
    gn_gain,
    gn_bias,
    cam_idx,
    noise_idx,
    cam_table,
    noise_table,
    conv_w,
    conv_bias,
    ln_gain,
    attn_in,
    attn_out,
    head_scale,
):
    _, _, rows, W, C = latent.shape
    V = lax.axis_size("view")
    R = lax.axis_size("row")
    heads = head_scale.shape[0]
    head = C // heads
    H = math.gcd(V, heads)
    g = V // H
    Wp = up(W + 1, 16)
    B = rows * Wp
    T = up(-(-B // g), 16)
    Cr = conv_w.shape[-1]
    width = C // H

    film = lax.dynamic_slice_in_dim(
        cam_table, cam_idx[0, 0], 1, 0, allow_negative_indices=False
    ).astype(F32) + lax.dynamic_slice_in_dim(
        noise_table, noise_idx[0], 1, 0, allow_negative_indices=False
    ).astype(F32)

    dma = pltpu.SemaphoreType.DMA
    vmem = pl.BlockSpec(memory_space=pltpu.VMEM)
    smem = pl.BlockSpec(memory_space=pltpu.SMEM)
    hbm = pl.BlockSpec(memory_space=pl.ANY)
    out = pl.pallas_call(
        functools.partial(kernel, (V, R, H, g, T, rows, W, Wp, C, head)),
        out_shape=jax.ShapeDtypeStruct((rows, W, C), BF16),
        in_specs=[vmem] * 6 + [smem] + [hbm] * 3,
        out_specs=vmem,
        scratch_shapes=[
            pltpu.VMEM((R, 2, C), F32),
            pltpu.VMEM((R * B, C), BF16),
            pltpu.VMEM((3, 3 * Cr, C), BF16),
            pltpu.VMEM((R * B + 2 * Wp, 3 * Cr), F32),
            pltpu.VMEM((R, B, Cr), BF16),
            pltpu.VMEM((R, B, Cr), BF16),
            pltpu.VMEM((3, C // H, C), BF16),
            pltpu.VMEM((C, C), BF16),
            pltpu.VMEM((g * T, C), BF16),
            pltpu.VMEM((g, H, T, C), BF16),
            pltpu.VMEM((3, V * T, width), F32),
            pltpu.VMEM((V, T, width), BF16),
            pltpu.VMEM((H, g * T, width), BF16),
            pltpu.VMEM((B, C), BF16),
            pltpu.VMEM((2, V * T, width), BF16),
            pltpu.VMEM((2 * V * T, 128), F32),
            pltpu.VMEM((V * T, 128), BF16),
            pltpu.VMEM((V * T, width), F32),
            dma((3,)),
            dma((R,)),
            dma((R,)),
            dma((R,)),
            dma((R,)),
            dma((R,)),
            dma((R,)),
            dma((R,)),
            dma((R,)),
            dma((g,)),
            dma((g,)),
            dma((g,)),
            dma((g,)),
            dma((g,)),
            dma((g,)),
            dma((3, g)),
            dma((3, g)),
            dma((V,)),
            dma((V,)),
            dma((g,)),
            dma((g,)),
            dma((3, g)),
            dma((3, g)),
            dma((V,)),
            dma((V,)),
            dma((g,)),
            dma((g,)),
            dma((V,)),
            dma((V,)),
        ],
        compiler_params=pltpu.CompilerParams(
            collective_id=0, has_side_effects=True, vmem_limit_bytes=56 * 2**20
        ),
        cost_estimate=pl.CostEstimate(
            flops=2 * R * B * C * Cr * 9, bytes_accessed=40_000_000, transcendentals=0
        ),
    )(
        latent.reshape(rows, W, C),
        film,
        gn_gain,
        gn_bias,
        conv_bias,
        ln_gain,
        head_scale,
        jnp.swapaxes(conv_w, 2, 3).reshape(3, 3 * Cr, C),
        jnp.swapaxes(attn_in, 1, 2),
        attn_out,
    )
    return out.reshape(latent.shape)


def solution(mesh):
    placed = (
        P(None, "view", "row", None, None),
        P(),
        P(),
        P(None, "view"),
        P(),
        P(),
        P(),
        P(None, None, None, "row"),
        P(),
        P(),
        P(None, None, "view"),
        P("view", None),
        P(),
    )
    return jax.shard_map(
        local,
        mesh=mesh,
        in_specs=placed,
        out_specs=P(None, "view", "row", None, None),
        check_vma=False,
    )
```

```python
import functools
import math

import jax
import jax.numpy as jnp
from jax import lax
from jax.experimental import pallas as pl
from jax.experimental.pallas import tpu as pltpu
from jax.sharding import PartitionSpec as P

GROUPS = 32
EPS = 1e-05
F32 = jnp.float32
BF16 = jnp.bfloat16


def up(n, m):
    return (n + m - 1) // m * m


def dot_t(a, b):
    return lax.dot_general(a, b, (((1,), (1,)), ((), ())), preferred_element_type=F32)


def one_hot(shape, long_axis, size):
    long = lax.broadcasted_iota(jnp.int32, shape, long_axis)
    short = lax.broadcasted_iota(jnp.int32, shape, 1 - long_axis) * size
    return (long >= short) & (long < short + size)


def kernel(
    dims,
    x_ref,
    film_ref,
    gn_gain_ref,
    gn_bias_ref,
    conv_bias_ref,
    ln_gain_ref,
    scale_ref,
    conv_hbm,
    attn_hbm,
    proj_hbm,
    out_ref,
    stat,
    act,
    conv_w,
    acc,
    conv_s,
    conv_r,
    attn_w,
    proj_w,
    ny,
    ally,
    qkv,
    mix_s,
    mix_r,
    resid_s,
    pieces,
    scores,
    soft,
    wide,
    load_sem,
    stat_ss,
    stat_rs,
    act_ss,
    act_rs,
    fwd_ss,
    fwd_rs,
    conv_ss,
    conv_rs,
    attn_ss,
    attn_rs,
    attn_fs,
    attn_fr,
    pair_ss,
    pair_rs,
    line_ss,
    line_rs,
    mix_ss,
    mix_rs,
    cross_ss,
    cross_rs,
    proj_ss,
    proj_rs,
    proj_fs,
    proj_fr,
    attn_xs,
    attn_xr,
    proj_xs,
    proj_xr,
):
    V, R, H, g, T, rows, W, Wp, C, head = dims
    B = rows * Wp
    Cr = conv_w.shape[1] // 3
    v = lax.axis_index("view")
    r = lax.axis_index("row")
    h = v % H
    q = v // H
    core = r % 2
    sib = r + 1 - 2 * core

    def at(view=None, row=None):
        return (v if view is None else view, r if row is None else row)

    def remote(src, dst, ss, rs, device):
        return pltpu.make_async_remote_copy(
            src_ref=src,
            dst_ref=dst,
            send_sem=ss,
            recv_sem=rs,
            device_id=device,
            device_id_type=pl.DeviceIdType.MESH,
        )

    load_conv = pltpu.make_async_copy(conv_hbm, conv_w, load_sem.at[0])
    Ca = proj_hbm.shape[0]
    half = C // 2
    mine = pl.ds(pl.multiple_of(core * half, half), half)

    nx = 2 if R == 4 and Ca % 32 == 0 else 1
    Cq = Ca // nx
    first = (r // 2) % nx * Cq
    across = (r + 2) % R

    def proj_block(view, columns):
        return proj_w.at[pl.ds(pl.multiple_of(view * Ca, 16), Ca), columns]

    def proj_quarter(view):
        return proj_w.at[pl.ds(pl.multiple_of(view * Ca + first, 16), Cq), mine]

    load_proj = pltpu.make_async_copy(proj_hbm, proj_block(v, slice(None)), load_sem.at[2])
    load_proj.start()
    load_conv.start()
    barrier = pltpu.get_barrier_semaphore()
    for o in range(1, R):
        pl.semaphore_signal(
            barrier, inc=1, device_id=at(row=(r + o) % R), device_id_type=pl.DeviceIdType.MESH
        )
    for o in range(1, V):
        pl.semaphore_signal(
            barrier, inc=1, device_id=at(view=(v + o) % V), device_id_type=pl.DeviceIdType.MESH
        )

    lanes = [slice(k, min(k + 256, C)) for k in range(0, C, 256)]
    size = C // GROUPS
    into = one_hot((C, 128), 0, size).astype(F32).astype(BF16)
    back = one_hot((128, C), 1, size).astype(F32).astype(BF16)
    count = rows * W * size

    def sum_dot(values, ones):
        line = lax.broadcasted_iota(jnp.int32, (8, values.shape[1]), 0)
        values = jnp.broadcast_to(values, line.shape)
        top = values.astype(BF16).astype(F32)
        rest = values - top
        middle = rest.astype(BF16).astype(F32)
        low = rest - middle
        pieces = jnp.where(line == 0, top, jnp.where(line == 1, middle, low))
        pieces = jnp.where(line < 3, pieces, 0.0).astype(BF16)
        return jnp.sum(
            jnp.dot(pieces, ones, preferred_element_type=F32), axis=0, keepdims=True
        )

    def spread(total):
        return sum_dot(sum_dot(total, into), back)

    def by_lanes(total):
        parts = []
        for part in lanes:
            parts.append(sum(total(x_ref[i, :, part].astype(F32), part) for i in range(rows)))
        return jnp.concatenate(parts, axis=1)

    def squares(x, part):
        off = x - mean_here[:, part]
        return jnp.sum(off * off, axis=0, keepdims=True)

    mean_here = spread(by_lanes(lambda x, part: jnp.sum(x, axis=0, keepdims=True)))
    mean_here = mean_here * (1.0 / count)
    square_here = spread(by_lanes(squares))
    stat[r, 0:1, :] = mean_here
    stat[r, 1:2, :] = square_here

    pl.semaphore_wait(barrier, R - 1 + V - 1)

    stat_copies = []
    for o in range(1, R):
        copy = remote(
            stat.at[r], stat.at[r], stat_ss.at[o], stat_rs.at[o], at(row=(r + o) % R)
        )
        copy.start()
        stat_copies.append(copy)

    beside = h + 1 - 2 * (h % 2)
    above = (h + 2) % H

    def view_of(part, group):
        return part * H + group

    def hop(slot, ss, rs, way, o):
        part = slot((q + g - o) % g, above if way == 2 else h)
        return remote(
            part,
            part,
            ss.at[way, o],
            rs.at[way, o],
            at(view=view_of(q, above if way == 1 else beside)),
        )

    def proj_slot(part, group):
        return proj_quarter(view_of(part, group))

    proj_hop = functools.partial(hop, proj_slot, proj_ss, proj_rs)
    load_proj.wait()
    proj_hop(1, 0).start()
    proj_hop(0, 0).start()
    cross_copies = []
    for o in range(1, g):
        copy = remote(
            proj_slot(q, h),
            proj_slot(q, h),
            cross_ss.at[o],
            cross_rs.at[o],
            at(view=view_of((q + o) % g, h)),
        )
        copy.start()
        cross_copies.append(copy)

    def shard(k, columns):
        return attn_w.at[:, pl.ds(pl.multiple_of(k * Ca, 16), Ca), columns]

    def attn_quarter(k):
        return attn_w.at[:, pl.ds(pl.multiple_of(k * Ca + first, 16), Cq), mine]

    def attn_send(k):
        return remote(
            attn_hbm.at[:, pl.ds(pl.multiple_of(first, 16), Cq), mine],
            attn_quarter(v % g),
            attn_ss.at[k],
            attn_rs.at[v % g],
            at(view=v // g + H * k),
        )

    load_attn = pltpu.make_async_copy(attn_hbm, shard(v % g, slice(None)), load_sem.at[1])
    for k in range(g):
        here = v // g + H * k == v

        @pl.when(here)
        def _():
            load_attn.start()

        @pl.when(jnp.logical_not(here))
        def _():
            attn_send(k).start()

    for copy in stat_copies:
        copy.wait()
    means = [stat[d, 0:1, :] for d in range(R)]
    mean = sum(means[1:], means[0]) * (1.0 / R)
    total = jnp.zeros((1, C), F32)
    for d in range(R):
        gap = means[d] - mean
        total = total + stat[d, 1:2, :] + count * (gap * gap)
    rstd = lax.rsqrt(total * (1.0 / (count * R)) + EPS)
    film_gain = 1.0 + film_ref[:, :C]
    gain = rstd * (gn_gain_ref[...].reshape(1, C) * film_gain)
    shift = gn_bias_ref[...].reshape(1, C) * film_gain + film_ref[:, C:]
    none = jnp.zeros((Wp - W, 256), F32)
    for i in range(rows):
        for part in lanes:
            x = x_ref[i, :, part].astype(F32)
            hidden = (x - mean[:, part]) * gain[:, part] + shift[:, part]
            hidden = hidden / (1.0 + jnp.exp(-hidden))
            hidden = jnp.concatenate([hidden, none[:, : hidden.shape[1]]], axis=0)
            line = pl.ds(pl.multiple_of(B * r + i * Wp, 16), Wp)
            act[line, part] = hidden.astype(BF16)

    def block(d):
        return act.at[pl.ds(pl.multiple_of(B * d, 16), B), :]

    act_copies = []
    for o in range(1, R // 2):
        copy = remote(
            block(r), block(r), act_ss.at[o], act_rs.at[o], at(row=(r + 2 * o) % R)
        )
        copy.start()
        act_copies.append(copy)
    forwards = [remote(block(r), block(r), fwd_ss.at[0], fwd_rs.at[0], at(row=sib))]
    forwards[0].start()

    for o in range(1, g):
        cross_copies[o - 1].wait()
        proj_hop(1, o).start()
        proj_hop(0, o).start()
    proj_hop(1, 0).wait_recv()
    proj_hop(2, 0).start()

    acc[...] = jnp.zeros(acc.shape, F32)

    def convolve(pair):
        start = pl.multiple_of(pair * 2 * B, 16)

        def taps(i, carry):
            lines = act[pl.ds(start, 2 * B), :]
            out = pl.ds(pl.multiple_of(start + (2 - i) * Wp, 16), 2 * B)
            acc[out, :] += dot_t(lines, conv_w[i])
            return carry

        lax.fori_loop(0, 3, taps, 0)

    load_conv.wait()
    forwards[0].wait_recv()
    convolve(r // 2)
    for o in range(1, g):
        proj_hop(1, o).wait_recv()
        proj_hop(2, o).start()
    for o in range(1, R // 2):
        act_copies[o - 1].wait_recv()
        source = (r + R - 2 * o) % R
        copy = remote(
            block(source), block(source), fwd_ss.at[o], fwd_rs.at[o], at(row=sib)
        )
        copy.start()
        forwards.append(copy)
    for o in range(1, R // 2):
        forwards[o].wait_recv()
        convolve((r // 2 + R // 2 - o) % (R // 2))

    for copy in act_copies + forwards:
        copy.wait_send()

    def combine(d):
        sums = acc[pl.ds(pl.multiple_of(B * d + Wp, 16), B), :]
        left = sums[:, :Cr]
        left = jnp.concatenate([left[B - 1 :], left[: B - 1]], axis=0)
        right = sums[:, 2 * Cr :]
        right = jnp.concatenate([right[1:], right[:1]], axis=0)
        return (left + sums[:, Cr : 2 * Cr] + right).astype(BF16)

    def conv_send(o):
        return remote(
            conv_s.at[o], conv_r.at[r], conv_ss.at[o], conv_rs.at[o], at(row=(r + o) % R)
        )

    def return_block(o, carry):
        conv_s[o] = combine((r + o) % R)
        conv_send(o).start()
        return carry

    lax.fori_loop(1, R, return_block, 0)
    conv_r[r] = combine(r)
    for i in range(rows):
        resid_s[i * Wp : i * Wp + W, :] = x_ref[i]
        resid_s[i * Wp + W : (i + 1) * Wp, :] = jnp.zeros((Wp - W, C), BF16)
    conv_copies = [conv_send(o) for o in range(1, R)]

    def attn_arrived(k):
        part = attn_quarter(k)
        return remote(part, part, attn_ss.at[k], attn_rs.at[k], at(view=(v + 1) % V))

    def attn_across(k):
        part = attn_quarter(k)
        return remote(part, part, attn_xs.at[k], attn_xr.at[k], at(row=across))

    def attn_forward(k):
        part = shard(k, mine)
        return remote(part, part, attn_fs.at[k], attn_fr.at[k], at(row=sib))

    for copy in conv_copies:
        copy.wait()
    for k in range(g):

        @pl.when(g * h + k != v)
        def _():
            attn_arrived(k).wait_recv()
            if nx > 1:
                attn_across(k).start()

    bias = conv_bias_ref[...].reshape(1, C)
    scale_y = ln_gain_ref[...].reshape(1, C)
    for start in range(0, B, 16):
        lines = slice(start, start + 16)
        conv = jnp.concatenate([conv_r[d, lines, :].astype(F32) for d in range(R)], axis=1)
        resid = (resid_s[lines, :].astype(F32) + conv + bias).astype(BF16)
        resid_s[lines, :] = resid
        resid = resid.astype(F32)
        middle = jnp.mean(resid, axis=1, keepdims=True)
        gap = resid - middle
        var = jnp.mean(gap * gap, axis=1, keepdims=True)
        ny[lines, :] = (gap * lax.rsqrt(var + EPS) * scale_y).astype(BF16)
    if g * T > B:
        ny[B : g * T, :] = jnp.zeros((g * T - B, C), BF16)

    def share(k):
        return pl.ds(pl.multiple_of(k * T, 16), T)

    ally[q, h] = ny[share(q), :]
    pair_copies = []
    for o in range(1, g):
        to = (q + o) % g
        copy = remote(
            ny.at[share(to), :], ally.at[q, h], pair_ss.at[o], pair_rs.at[o], at(view=view_of(to, h))
        )
        copy.start()
        pair_copies.append(copy)

    line_hop = functools.partial(hop, lambda part, group: ally.at[part, group], line_ss, line_rs)
    line_hop(1, 0).start()
    line_hop(0, 0).start()
    for o in range(1, g):
        line_hop(1, o - 1).wait_recv()
        line_hop(2, o - 1).start()
        pair_copies[o - 1].wait_recv()
        line_hop(1, o).start()
        line_hop(0, o).start()
    line_hop(1, g - 1).wait_recv()
    line_hop(2, g - 1).start()
    for o in range(g):
        proj_hop(0, o).wait()
        proj_hop(1, o).wait_send()
        proj_hop(2, o).wait()

    def proj_across(o):
        part = proj_quarter((v + o) % V)
        return remote(part, part, proj_xs.at[o], proj_xr.at[o], at(row=across))

    def proj_forward(o):
        part = proj_block((v + o) % V, mine)
        return remote(part, part, proj_fs.at[o], proj_fr.at[o], at(row=sib))

    for k in range(g):

        @pl.when(g * h + k != v)
        def _():
            if nx > 1:
                attn_across(k).wait()
            attn_forward(k).start()

    if nx > 1:
        for o in range(1, V):
            proj_across(o).start()

    for k in range(g):
        here = v // g + H * k == v

        @pl.when(here)
        def _():
            load_attn.wait()

        @pl.when(jnp.logical_not(here))
        def _():
            attn_send(k).wait_send()

        @pl.when(g * h + k != v)
        def _():
            attn_forward(k).wait()

    for copy in pair_copies:
        copy.wait_send()
    width = qkv.shape[-1]
    for o in range(g):
        line_hop(0, o).wait()
        line_hop(1, o).wait_send()
        line_hop(2, o).wait()
        part = (q + g - o) % g
        lines = ally[part].reshape(H * T, C)
        place = pl.ds(pl.multiple_of(part * (H * T), 16), H * T)
        for kind in range(3):
            qkv[kind, place, :] = dot_t(lines, attn_w[kind]).astype(BF16).astype(F32)

    into_heads = one_hot((width, 128), 0, head).astype(BF16)
    from_heads = one_hot((128, width), 1, head).astype(BF16)
    lane = lax.broadcasted_iota(jnp.int32, (1, 128), 1)
    scale = jnp.zeros((1, 128), F32)
    for k in range(width // head):
        scale = jnp.where(lane == k, scale_ref[h * (width // head) + k], scale)
    scale = scale * (1.0 / math.sqrt(head))

    def attend(k, carry):
        u = view_of((q + 1 + k // H) % g, (h + 1 + k) % H)
        base = pl.multiple_of(u * T, 16)
        for start in range(0, T, 16):
            query = qkv[0, pl.ds(base + start, 16), :]
            for w in range(V):
                lines = slice(w * T + start, w * T + start + 16)
                product = query * qkv[1, lines, :]
                top = product.astype(BF16)
                pieces[0, lines, :] = top
                pieces[1, lines, :] = (product - top.astype(F32)).astype(BF16)
        scores[...] = jnp.dot(
            pieces[...].reshape(2 * V * T, width), into_heads, preferred_element_type=F32
        )
        for start in range(0, T, 16):
            several = []
            for w in range(V):
                line = w * T + start
                several.append(
                    (scores[line : line + 16] + scores[V * T + line : V * T + line + 16]) * scale
                )
            peak = functools.reduce(jnp.maximum, several)
            several = [jnp.exp(one - peak) for one in several]
            inverse = 1.0 / sum(several)
            for w in range(V):
                line = w * T + start
                soft[line : line + 16] = (several[w] * inverse).astype(BF16)
        wide[...] = jnp.dot(soft[...], from_heads, preferred_element_type=F32)
        mixed = []
        for start in range(0, T, 16):
            total = 0.0
            for w in range(V):
                lines = slice(w * T + start, w * T + start + 16)
                total = total + wide[lines, :] * qkv[2, lines, :]
            mixed.append(total.astype(BF16))
        mixed = jnp.concatenate(mixed, axis=0)

        @pl.when(u == v)
        def _():
            mix_r[h, share(q), :] = mixed

        @pl.when(u != v)
        def _():
            mix_s[u] = mixed
            remote(
                mix_s.at[u],
                mix_r.at[h, share(q), :],
                mix_ss.at[u],
                mix_rs.at[v],
                at(view=u),
            ).start()

        return carry

    lax.fori_loop(0, V // 2, attend, 0)
    for o in range(1, V):
        if nx > 1:
            proj_across(o).wait()
        proj_forward(o).start()
    lax.fori_loop(V // 2, V, attend, 0)

    def finish(k, carry):
        u = (v + 1 + k) % V
        remote(
            mix_s.at[u],
            mix_r.at[u % H, share(u // H), :],
            mix_ss.at[u],
            mix_rs.at[u],
            at(view=u),
        ).wait()
        return carry

    lax.fori_loop(0, V - 1, finish, 0)
    for o in range(1, V):
        proj_forward(o).wait()
    mixed = jnp.concatenate([mix_r[k].astype(F32) for k in range(H)], axis=1).astype(BF16)
    projected = jnp.dot(mixed[:B], proj_w[...], preferred_element_type=F32)
    for i in range(rows):
        out_ref[i] = (
            resid_s[i * Wp : i * Wp + W].astype(F32) + projected[i * Wp : i * Wp + W]
        ).astype(BF16)


def local(
    latent,
    gn_gain,
    gn_bias,
    cam_idx,
    noise_idx,
    cam_table,
    noise_table,
    conv_w,
    conv_bias,
    ln_gain,
    attn_in,
    attn_out,
    head_scale,
):
    _, _, rows, W, C = latent.shape
    V = lax.axis_size("view")
    R = lax.axis_size("row")
    heads = head_scale.shape[0]
    head = C // heads
    H = math.gcd(V, heads)
    g = V // H
    Wp = up(W + 1, 16)
    B = rows * Wp
    T = up(-(-B // g), 16)
    Cr = conv_w.shape[-1]
    width = C // H

    film = lax.dynamic_slice_in_dim(
        cam_table, cam_idx[0, 0], 1, 0, allow_negative_indices=False
    ).astype(F32) + lax.dynamic_slice_in_dim(
        noise_table, noise_idx[0], 1, 0, allow_negative_indices=False
    ).astype(F32)

    dma = pltpu.SemaphoreType.DMA
    vmem = pl.BlockSpec(memory_space=pltpu.VMEM)
    smem = pl.BlockSpec(memory_space=pltpu.SMEM)
    hbm = pl.BlockSpec(memory_space=pl.ANY)
    out = pl.pallas_call(
        functools.partial(kernel, (V, R, H, g, T, rows, W, Wp, C, head)),
        out_shape=jax.ShapeDtypeStruct((rows, W, C), BF16),
        in_specs=[vmem] * 6 + [smem] + [hbm] * 3,
        out_specs=vmem,
        scratch_shapes=[
            pltpu.VMEM((R, 2, C), F32),
            pltpu.VMEM((R * B, C), BF16),
            pltpu.VMEM((3, 3 * Cr, C), BF16),
            pltpu.VMEM((R * B + 2 * Wp, 3 * Cr), F32),
            pltpu.VMEM((R, B, Cr), BF16),
            pltpu.VMEM((R, B, Cr), BF16),
            pltpu.VMEM((3, C // H, C), BF16),
            pltpu.VMEM((C, C), BF16),
            pltpu.VMEM((g * T, C), BF16),
            pltpu.VMEM((g, H, T, C), BF16),
            pltpu.VMEM((3, V * T, width), F32),
            pltpu.VMEM((V, T, width), BF16),
            pltpu.VMEM((H, g * T, width), BF16),
            pltpu.VMEM((B, C), BF16),
            pltpu.VMEM((2, V * T, width), BF16),
            pltpu.VMEM((2 * V * T, 128), F32),
            pltpu.VMEM((V * T, 128), BF16),
            pltpu.VMEM((V * T, width), F32),
            dma((3,)),
            dma((R,)),
            dma((R,)),
            dma((R,)),
            dma((R,)),
            dma((R,)),
            dma((R,)),
            dma((R,)),
            dma((R,)),
            dma((g,)),
            dma((g,)),
            dma((g,)),
            dma((g,)),
            dma((g,)),
            dma((g,)),
            dma((3, g)),
            dma((3, g)),
            dma((V,)),
            dma((V,)),
            dma((g,)),
            dma((g,)),
            dma((3, g)),
            dma((3, g)),
            dma((V,)),
            dma((V,)),
            dma((g,)),
            dma((g,)),
            dma((V,)),
            dma((V,)),
        ],
        compiler_params=pltpu.CompilerParams(
            collective_id=0, has_side_effects=True, vmem_limit_bytes=56 * 2**20
        ),
        cost_estimate=pl.CostEstimate(
            flops=2 * R * B * C * Cr * 9, bytes_accessed=40_000_000, transcendentals=0
        ),
    )(
        latent.reshape(rows, W, C),
        film,
        gn_gain,
        gn_bias,
        conv_bias,
        ln_gain,
        head_scale,
        jnp.swapaxes(conv_w, 2, 3).reshape(3, 3 * Cr, C),
        jnp.swapaxes(attn_in, 1, 2),
        attn_out,
    )
    return out.reshape(latent.shape)


def solution(mesh):
    placed = (
        P(None, "view", "row", None, None),
        P(),
        P(),
        P(None, "view"),
        P(),
        P(),
        P(),
        P(None, None, None, "row"),
        P(),
        P(),
        P(None, None, "view"),
        P("view", None),
        P(),
    )
    return jax.shard_map(
        local,
        mesh=mesh,
        in_specs=placed,
        out_specs=P(None, "view", "row", None, None),
        check_vma=False,
    )
```

```python
import functools
import math

import jax
import jax.numpy as jnp
from jax import lax
from jax.experimental import pallas as pl
from jax.experimental.pallas import tpu as pltpu
from jax.sharding import PartitionSpec as P

GROUPS = 32
EPS = 1e-05
F32 = jnp.float32
BF16 = jnp.bfloat16


def up(n, m):
    return (n + m - 1) // m * m


def dot_t(a, b):
    return lax.dot_general(a, b, (((1,), (1,)), ((), ())), preferred_element_type=F32)


def one_hot(shape, long_axis, size):
    long = lax.broadcasted_iota(jnp.int32, shape, long_axis)
    short = lax.broadcasted_iota(jnp.int32, shape, 1 - long_axis) * size
    return (long >= short) & (long < short + size)


def kernel(
    dims,
    x_ref,
    film_ref,
    gn_gain_ref,
    gn_bias_ref,
    conv_bias_ref,
    ln_gain_ref,
    scale_ref,
    conv_hbm,
    attn_hbm,
    proj_hbm,
    out_ref,
    stat,
    act,
    conv_w,
    acc,
    conv_s,
    conv_r,
    attn_w,
    proj_w,
    ny,
    ally,
    qkv,
    mix_s,
    mix_r,
    resid_s,
    pieces,
    scores,
    soft,
    wide,
    load_sem,
    stat_ss,
    stat_rs,
    act_ss,
    act_rs,
    fwd_ss,
    fwd_rs,
    conv_ss,
    conv_rs,
    attn_ss,
    attn_rs,
    attn_fs,
    attn_fr,
    pair_ss,
    pair_rs,
    line_ss,
    line_rs,
    mix_ss,
    mix_rs,
    cross_ss,
    cross_rs,
    proj_ss,
    proj_rs,
    proj_fs,
    proj_fr,
    attn_xs,
    attn_xr,
    proj_xs,
    proj_xr,
):
    V, R, H, g, T, rows, W, Wp, C, head = dims
    B = rows * Wp
    Cr = conv_w.shape[1] // 3
    v = lax.axis_index("view")
    r = lax.axis_index("row")
    h = v % H
    q = v // H
    core = r % 2
    sib = r + 1 - 2 * core

    def at(view=None, row=None):
        return (v if view is None else view, r if row is None else row)

    def remote(src, dst, ss, rs, device):
        return pltpu.make_async_remote_copy(
            src_ref=src,
            dst_ref=dst,
            send_sem=ss,
            recv_sem=rs,
            device_id=device,
            device_id_type=pl.DeviceIdType.MESH,
        )

    load_conv = pltpu.make_async_copy(conv_hbm, conv_w, load_sem.at[0])
    Ca = proj_hbm.shape[0]
    half = C // 2
    mine = pl.ds(pl.multiple_of(core * half, half), half)

    nx = 2 if R == 4 and Ca % 32 == 0 else 1
    Cq = Ca // nx
    first = (r // 2) % nx * Cq
    across = (r + 2) % R

    def proj_block(view, columns):
        return proj_w.at[pl.ds(pl.multiple_of(view * Ca, 16), Ca), columns]

    def proj_quarter(view):
        return proj_w.at[pl.ds(pl.multiple_of(view * Ca + first, 16), Cq), mine]

    load_proj = pltpu.make_async_copy(proj_hbm, proj_block(v, slice(None)), load_sem.at[2])
    load_proj.start()
    load_conv.start()
    barrier = pltpu.get_barrier_semaphore()
    for o in range(1, R):
        pl.semaphore_signal(
            barrier, inc=1, device_id=at(row=(r + o) % R), device_id_type=pl.DeviceIdType.MESH
        )
    for o in range(1, V):
        pl.semaphore_signal(
            barrier, inc=1, device_id=at(view=(v + o) % V), device_id_type=pl.DeviceIdType.MESH
        )

    lanes = [slice(k, min(k + 256, C)) for k in range(0, C, 256)]
    size = C // GROUPS
    into = one_hot((C, 128), 0, size).astype(F32).astype(BF16)
    back = one_hot((128, C), 1, size).astype(F32).astype(BF16)
    count = rows * W * size

    def sum_dot(values, ones):
        line = lax.broadcasted_iota(jnp.int32, (8, values.shape[1]), 0)
        values = jnp.broadcast_to(values, line.shape)
        top = values.astype(BF16).astype(F32)
        rest = values - top
        middle = rest.astype(BF16).astype(F32)
        low = rest - middle
        pieces = jnp.where(line == 0, top, jnp.where(line == 1, middle, low))
        pieces = jnp.where(line < 3, pieces, 0.0).astype(BF16)
        return jnp.sum(
            jnp.dot(pieces, ones, preferred_element_type=F32), axis=0, keepdims=True
        )

    def spread(total):
        return sum_dot(sum_dot(total, into), back)

    def by_lanes(total):
        parts = []
        for part in lanes:
            parts.append(sum(total(x_ref[i, :, part].astype(F32), part) for i in range(rows)))
        return jnp.concatenate(parts, axis=1)

    def squares(x, part):
        off = x - mean_here[:, part]
        return jnp.sum(off * off, axis=0, keepdims=True)

    mean_here = spread(by_lanes(lambda x, part: jnp.sum(x, axis=0, keepdims=True)))
    mean_here = mean_here * (1.0 / count)
    square_here = spread(by_lanes(squares))
    stat[r, 0:1, :] = mean_here
    stat[r, 1:2, :] = square_here

    pl.semaphore_wait(barrier, R - 1 + V - 1)

    stat_copies = []
    for o in range(1, R):
        copy = remote(
            stat.at[r], stat.at[r], stat_ss.at[o], stat_rs.at[o], at(row=(r + o) % R)
        )
        copy.start()
        stat_copies.append(copy)

    beside = h + 1 - 2 * (h % 2)
    above = (h + 2) % H

    def view_of(part, group):
        return part * H + group

    def hop(slot, ss, rs, way, o):
        part = slot((q + g - o) % g, above if way == 2 else h)
        return remote(
            part,
            part,
            ss.at[way, o],
            rs.at[way, o],
            at(view=view_of(q, above if way == 1 else beside)),
        )

    def proj_slot(part, group):
        return proj_quarter(view_of(part, group))

    proj_hop = functools.partial(hop, proj_slot, proj_ss, proj_rs)
    load_proj.wait()
    proj_hop(1, 0).start()
    proj_hop(0, 0).start()
    cross_copies = []
    for o in range(1, g):
        copy = remote(
            proj_slot(q, h),
            proj_slot(q, h),
            cross_ss.at[o],
            cross_rs.at[o],
            at(view=view_of((q + o) % g, h)),
        )
        copy.start()
        cross_copies.append(copy)

    def shard(k, columns):
        return attn_w.at[:, pl.ds(pl.multiple_of(k * Ca, 16), Ca), columns]

    def attn_quarter(k):
        return attn_w.at[:, pl.ds(pl.multiple_of(k * Ca + first, 16), Cq), mine]

    def attn_send(k):
        return remote(
            attn_hbm.at[:, pl.ds(pl.multiple_of(first, 16), Cq), mine],
            attn_quarter(v % g),
            attn_ss.at[k],
            attn_rs.at[v % g],
            at(view=v // g + H * k),
        )

    load_attn = pltpu.make_async_copy(attn_hbm, shard(v % g, slice(None)), load_sem.at[1])
    for k in range(g):
        here = v // g + H * k == v

        @pl.when(here)
        def _():
            load_attn.start()

        @pl.when(jnp.logical_not(here))
        def _():
            attn_send(k).start()

    for copy in stat_copies:
        copy.wait()
    means = [stat[d, 0:1, :] for d in range(R)]
    mean = sum(means[1:], means[0]) * (1.0 / R)
    total = jnp.zeros((1, C), F32)
    for d in range(R):
        gap = means[d] - mean
        total = total + stat[d, 1:2, :] + count * (gap * gap)
    rstd = lax.rsqrt(total * (1.0 / (count * R)) + EPS)
    film_gain = 1.0 + film_ref[:, :C]
    gain = rstd * (gn_gain_ref[...].reshape(1, C) * film_gain)
    shift = gn_bias_ref[...].reshape(1, C) * film_gain + film_ref[:, C:]
    none = jnp.zeros((Wp - W, 256), F32)
    for i in range(rows):
        for part in lanes:
            x = x_ref[i, :, part].astype(F32)
            hidden = (x - mean[:, part]) * gain[:, part] + shift[:, part]
            hidden = hidden / (1.0 + jnp.exp(-hidden))
            hidden = jnp.concatenate([hidden, none[:, : hidden.shape[1]]], axis=0)
            line = pl.ds(pl.multiple_of(B * r + i * Wp, 16), Wp)
            act[line, part] = hidden.astype(BF16)

    def block(d):
        return act.at[pl.ds(pl.multiple_of(B * d, 16), B), :]

    act_copies = []
    for o in range(1, R // 2):
        copy = remote(
            block(r), block(r), act_ss.at[o], act_rs.at[o], at(row=(r + 2 * o) % R)
        )
        copy.start()
        act_copies.append(copy)
    forwards = [remote(block(r), block(r), fwd_ss.at[0], fwd_rs.at[0], at(row=sib))]
    forwards[0].start()

    for o in range(1, g):
        cross_copies[o - 1].wait()
        proj_hop(1, o).start()
        proj_hop(0, o).start()
    proj_hop(1, 0).wait_recv()
    proj_hop(2, 0).start()

    acc[...] = jnp.zeros(acc.shape, F32)

    def convolve(pair):
        start = pl.multiple_of(pair * 2 * B, 16)

        def taps(i, carry):
            lines = act[pl.ds(start, 2 * B), :]
            out = pl.ds(pl.multiple_of(start + (2 - i) * Wp, 16), 2 * B)
            acc[out, :] += dot_t(lines, conv_w[i])
            return carry

        lax.fori_loop(0, 3, taps, 0)

    load_conv.wait()
    forwards[0].wait_recv()
    convolve(r // 2)
    for o in range(1, g):
        proj_hop(1, o).wait_recv()
        proj_hop(2, o).start()
    for o in range(1, R // 2):
        act_copies[o - 1].wait_recv()
        source = (r + R - 2 * o) % R
        copy = remote(
            block(source), block(source), fwd_ss.at[o], fwd_rs.at[o], at(row=sib)
        )
        copy.start()
        forwards.append(copy)
    for o in range(1, R // 2):
        forwards[o].wait_recv()
        convolve((r // 2 + R // 2 - o) % (R // 2))

    for copy in act_copies + forwards:
        copy.wait_send()

    def combine(d):
        sums = acc[pl.ds(pl.multiple_of(B * d + Wp, 16), B), :]
        left = sums[:, :Cr]
        left = jnp.concatenate([left[B - 1 :], left[: B - 1]], axis=0)
        right = sums[:, 2 * Cr :]
        right = jnp.concatenate([right[1:], right[:1]], axis=0)
        return (left + sums[:, Cr : 2 * Cr] + right).astype(BF16)

    def conv_send(o):
        return remote(
            conv_s.at[o], conv_r.at[r], conv_ss.at[o], conv_rs.at[o], at(row=(r + o) % R)
        )

    def return_block(o, carry):
        conv_s[o] = combine((r + o) % R)
        conv_send(o).start()
        return carry

    lax.fori_loop(1, R, return_block, 0)
    conv_r[r] = combine(r)
    for i in range(rows):
        resid_s[i * Wp : i * Wp + W, :] = x_ref[i]
        resid_s[i * Wp + W : (i + 1) * Wp, :] = jnp.zeros((Wp - W, C), BF16)
    conv_copies = [conv_send(o) for o in range(1, R)]

    def attn_arrived(k):
        part = attn_quarter(k)
        return remote(part, part, attn_ss.at[k], attn_rs.at[k], at(view=(v + 1) % V))

    def attn_across(k):
        part = attn_quarter(k)
        return remote(part, part, attn_xs.at[k], attn_xr.at[k], at(row=across))

    def attn_forward(k):
        part = shard(k, mine)
        return remote(part, part, attn_fs.at[k], attn_fr.at[k], at(row=sib))

    for k in range(g):

        @pl.when(g * h + k != v)
        def _():
            attn_arrived(k).wait_recv()
            if nx > 1:
                attn_across(k).start()

    for copy in conv_copies:
        copy.wait()
    bias = conv_bias_ref[...].reshape(1, C)
    scale_y = ln_gain_ref[...].reshape(1, C)
    for start in range(0, B, 16):
        lines = slice(start, start + 16)
        conv = jnp.concatenate([conv_r[d, lines, :].astype(F32) for d in range(R)], axis=1)
        resid = (resid_s[lines, :].astype(F32) + conv + bias).astype(BF16)
        resid_s[lines, :] = resid
        resid = resid.astype(F32)
        middle = jnp.mean(resid, axis=1, keepdims=True)
        gap = resid - middle
        var = jnp.mean(gap * gap, axis=1, keepdims=True)
        ny[lines, :] = (gap * lax.rsqrt(var + EPS) * scale_y).astype(BF16)
    if g * T > B:
        ny[B : g * T, :] = jnp.zeros((g * T - B, C), BF16)

    def share(k):
        return pl.ds(pl.multiple_of(k * T, 16), T)

    line_hop = functools.partial(hop, lambda part, group: ally.at[part, group], line_ss, line_rs)
    ally[q, h] = ny[share(q), :]
    line_hop(1, 0).start()
    line_hop(0, 0).start()
    pair_copies = []
    for o in range(1, g):
        to = (q + o) % g
        copy = remote(
            ny.at[share(to), :], ally.at[q, h], pair_ss.at[o], pair_rs.at[o], at(view=view_of(to, h))
        )
        copy.start()
        pair_copies.append(copy)

    for o in range(1, g):
        line_hop(1, o - 1).wait_recv()
        line_hop(2, o - 1).start()
        pair_copies[o - 1].wait_recv()
        line_hop(1, o).start()
        line_hop(0, o).start()
    line_hop(1, g - 1).wait_recv()
    line_hop(2, g - 1).start()
    for o in range(g):
        proj_hop(0, o).wait()
        proj_hop(1, o).wait_send()
        proj_hop(2, o).wait()

    def proj_across(o):
        part = proj_quarter((v + o) % V)
        return remote(part, part, proj_xs.at[o], proj_xr.at[o], at(row=across))

    def proj_forward(o):
        part = proj_block((v + o) % V, mine)
        return remote(part, part, proj_fs.at[o], proj_fr.at[o], at(row=sib))

    for k in range(g):

        @pl.when(g * h + k != v)
        def _():
            if nx > 1:
                attn_across(k).wait()
            attn_forward(k).start()

    if nx > 1:
        for o in range(1, V):
            proj_across(o).start()

    for k in range(g):
        here = v // g + H * k == v

        @pl.when(here)
        def _():
            load_attn.wait()

        @pl.when(jnp.logical_not(here))
        def _():
            attn_send(k).wait_send()

        @pl.when(g * h + k != v)
        def _():
            attn_forward(k).wait()

    for copy in pair_copies:
        copy.wait_send()
    width = qkv.shape[-1]
    for o in range(g):
        line_hop(0, o).wait()
        line_hop(1, o).wait_send()
        line_hop(2, o).wait()
        part = (q + g - o) % g
        lines = ally[part].reshape(H * T, C)
        place = pl.ds(pl.multiple_of(part * (H * T), 16), H * T)
        for kind in range(3):
            qkv[kind, place, :] = dot_t(lines, attn_w[kind]).astype(BF16).astype(F32)

    into_heads = one_hot((width, 128), 0, head).astype(BF16)
    from_heads = one_hot((128, width), 1, head).astype(BF16)
    lane = lax.broadcasted_iota(jnp.int32, (1, 128), 1)
    scale = jnp.zeros((1, 128), F32)
    for k in range(width // head):
        scale = jnp.where(lane == k, scale_ref[h * (width // head) + k], scale)
    scale = scale * (1.0 / math.sqrt(head))

    def attend(k, carry):
        u = (v + 1 + k) % V
        base = pl.multiple_of(u * T, 16)
        for start in range(0, T, 16):
            query = qkv[0, pl.ds(base + start, 16), :]
            for w in range(V):
                lines = slice(w * T + start, w * T + start + 16)
                product = query * qkv[1, lines, :]
                top = product.astype(BF16)
                pieces[0, lines, :] = top
                pieces[1, lines, :] = (product - top.astype(F32)).astype(BF16)
        scores[...] = jnp.dot(
            pieces[...].reshape(2 * V * T, width), into_heads, preferred_element_type=F32
        )
        for start in range(0, T, 16):
            several = []
            for w in range(V):
                line = w * T + start
                several.append(
                    (scores[line : line + 16] + scores[V * T + line : V * T + line + 16]) * scale
                )
            peak = functools.reduce(jnp.maximum, several)
            several = [jnp.exp(one - peak) for one in several]
            inverse = 1.0 / sum(several)
            for w in range(V):
                line = w * T + start
                soft[line : line + 16] = (several[w] * inverse).astype(BF16)
        wide[...] = jnp.dot(soft[...], from_heads, preferred_element_type=F32)
        mixed = []
        for start in range(0, T, 16):
            total = 0.0
            for w in range(V):
                lines = slice(w * T + start, w * T + start + 16)
                total = total + wide[lines, :] * qkv[2, lines, :]
            mixed.append(total.astype(BF16))
        mixed = jnp.concatenate(mixed, axis=0)

        @pl.when(u == v)
        def _():
            mix_r[h, share(q), :] = mixed

        @pl.when(u != v)
        def _():
            mix_s[u] = mixed
            remote(
                mix_s.at[u],
                mix_r.at[h, share(q), :],
                mix_ss.at[u],
                mix_rs.at[v],
                at(view=u),
            ).start()

        return carry

    lax.fori_loop(0, V // 2, attend, 0)
    for o in range(1, V):
        if nx > 1:
            proj_across(o).wait()
        proj_forward(o).start()
    lax.fori_loop(V // 2, V, attend, 0)

    def finish(k, carry):
        u = (v + 1 + k) % V
        remote(
            mix_s.at[u],
            mix_r.at[u % H, share(u // H), :],
            mix_ss.at[u],
            mix_rs.at[u],
            at(view=u),
        ).wait()
        return carry

    lax.fori_loop(0, V - 1, finish, 0)
    for o in range(1, V):
        proj_forward(o).wait()
    mixed = jnp.concatenate([mix_r[k].astype(F32) for k in range(H)], axis=1).astype(BF16)
    projected = jnp.dot(mixed[:B], proj_w[...], preferred_element_type=F32)
    for i in range(rows):
        out_ref[i] = (
            resid_s[i * Wp : i * Wp + W].astype(F32) + projected[i * Wp : i * Wp + W]
        ).astype(BF16)


def local(
    latent,
    gn_gain,
    gn_bias,
    cam_idx,
    noise_idx,
    cam_table,
    noise_table,
    conv_w,
    conv_bias,
    ln_gain,
    attn_in,
    attn_out,
    head_scale,
):
    _, _, rows, W, C = latent.shape
    V = lax.axis_size("view")
    R = lax.axis_size("row")
    heads = head_scale.shape[0]
    head = C // heads
    H = math.gcd(V, heads)
    g = V // H
    Wp = up(W + 1, 16)
    B = rows * Wp
    T = up(-(-B // g), 16)
    Cr = conv_w.shape[-1]
    width = C // H

    film = lax.dynamic_slice_in_dim(
        cam_table, cam_idx[0, 0], 1, 0, allow_negative_indices=False
    ).astype(F32) + lax.dynamic_slice_in_dim(
        noise_table, noise_idx[0], 1, 0, allow_negative_indices=False
    ).astype(F32)

    dma = pltpu.SemaphoreType.DMA
    vmem = pl.BlockSpec(memory_space=pltpu.VMEM)
    smem = pl.BlockSpec(memory_space=pltpu.SMEM)
    hbm = pl.BlockSpec(memory_space=pl.ANY)
    out = pl.pallas_call(
        functools.partial(kernel, (V, R, H, g, T, rows, W, Wp, C, head)),
        out_shape=jax.ShapeDtypeStruct((rows, W, C), BF16),
        in_specs=[vmem] * 6 + [smem] + [hbm] * 3,
        out_specs=vmem,
        scratch_shapes=[
            pltpu.VMEM((R, 2, C), F32),
            pltpu.VMEM((R * B, C), BF16),
            pltpu.VMEM((3, 3 * Cr, C), BF16),
            pltpu.VMEM((R * B + 2 * Wp, 3 * Cr), F32),
            pltpu.VMEM((R, B, Cr), BF16),
            pltpu.VMEM((R, B, Cr), BF16),
            pltpu.VMEM((3, C // H, C), BF16),
            pltpu.VMEM((C, C), BF16),
            pltpu.VMEM((g * T, C), BF16),
            pltpu.VMEM((g, H, T, C), BF16),
            pltpu.VMEM((3, V * T, width), F32),
            pltpu.VMEM((V, T, width), BF16),
            pltpu.VMEM((H, g * T, width), BF16),
            pltpu.VMEM((B, C), BF16),
            pltpu.VMEM((2, V * T, width), BF16),
            pltpu.VMEM((2 * V * T, 128), F32),
            pltpu.VMEM((V * T, 128), BF16),
            pltpu.VMEM((V * T, width), F32),
            dma((3,)),
            dma((R,)),
            dma((R,)),
            dma((R,)),
            dma((R,)),
            dma((R,)),
            dma((R,)),
            dma((R,)),
            dma((R,)),
            dma((g,)),
            dma((g,)),
            dma((g,)),
            dma((g,)),
            dma((g,)),
            dma((g,)),
            dma((3, g)),
            dma((3, g)),
            dma((V,)),
            dma((V,)),
            dma((g,)),
            dma((g,)),
            dma((3, g)),
            dma((3, g)),
            dma((V,)),
            dma((V,)),
            dma((g,)),
            dma((g,)),
            dma((V,)),
            dma((V,)),
        ],
        compiler_params=pltpu.CompilerParams(
            collective_id=0, has_side_effects=True, vmem_limit_bytes=56 * 2**20
        ),
        cost_estimate=pl.CostEstimate(
            flops=2 * R * B * C * Cr * 9, bytes_accessed=40_000_000, transcendentals=0
        ),
    )(
        latent.reshape(rows, W, C),
        film,
        gn_gain,
        gn_bias,
        conv_bias,
        ln_gain,
        head_scale,
        jnp.swapaxes(conv_w, 2, 3).reshape(3, 3 * Cr, C),
        jnp.swapaxes(attn_in, 1, 2),
        attn_out,
    )
    return out.reshape(latent.shape)


def solution(mesh):
    placed = (
        P(None, "view", "row", None, None),
        P(),
        P(),
        P(None, "view"),
        P(),
        P(),
        P(),
        P(None, None, None, "row"),
        P(),
        P(),
        P(None, None, "view"),
        P("view", None),
        P(),
    )
    return jax.shard_map(
        local,
        mesh=mesh,
        in_specs=placed,
        out_specs=P(None, "view", "row", None, None),
        check_vma=False,
    )
```
